512 devices in a mesh: layer: 32 (over x, y, core), dp: 16 (over z).
Axes of the slice: x: 4, y: 4, z: 16, core: 2. Of those that a mesh axis runs over, the one named last changes fastest.
Arguments:
- weights: bfloat16 [128, 512, 512], P('layer', 'dp'), may hold values from -0.25 to 0.25
- biases: float32 [128, 512], P('layer'), may hold values from -3 to 3
- guesses: float32 [32, 8192, 512], P('layer', 'dp'), may hold values from -6 to 6
Outputs:
- states: bfloat16 [128, 8192, 512], P('layer', 'dp')
The draws below stay inside these ranges and needn't reach their ends.
All inputs are finite; a program needn't handle non-finite values.
Results may differ from the reference program's by a relative error of at most 0.0041.
Values may be sent and summed in bfloat16 or wider, within the bound.
A program may use at most 64 MiB of HBM per device.

```python
import jax
import jax.numpy as jnp
from jax import lax

D = 512
L_DEV = 4
GROUP = 4
BLOCKS = 32
LAYERS = 128
BATCH = 8192
N_LAYER = 32


def levels(own_key, shape, shards, low, top_value):
    def one(axis_at, shards_of):
        steps = jax.random.uniform(jax.random.fold_in(jax.random.fold_in(own_key, 6), axis_at), (shards_of,), jnp.float32, low / len(shards), top_value / len(shards))
        return jnp.repeat(jnp.exp(steps), shape[axis_at] // shards_of).reshape((-1,) + (1,) * (len(shape) - axis_at - 1))

    level = one(*shards[0])
    for cut in shards[1:]:
        level = level * one(*cut)
    return level


def normal_values(key, extent, width, limit, shards=(), dtype=jnp.bfloat16):
    array = jax.random.normal(key, extent, jnp.float32) * width
    if len(shards) > 0:
        array = levels(key, extent, shards, -0.22, 0.18) * array
    return jnp.clip(array, min=-limit, max=limit).astype(dtype)


def setup_inputs(seed: int = 0) -> dict:
    key_of = jax.random.split(jax.random.key(seed), 4)
    return {
        "weights": normal_values(key_of[0], (LAYERS, D, D), D ** -0.5, 0.25, ((0, 32), (1, 16))),
        "biases": normal_values(key_of[1], (LAYERS, D), 0.5, 3.0, ((0, 32),), jnp.float32),
        "guesses": normal_values(key_of[2], (BLOCKS, BATCH, D), 1.0, 6.0, ((0, 32), (1, 16)), jnp.float32),
    }


def advance(states_in, weight_mat, bias_row, step_width):
    preact = jnp.dot(states_in.astype(jnp.bfloat16), weight_mat, preferred_element_type=jnp.float32)
    return states_in + step_width * jnp.tanh(preact + bias_row)


def advance_each(states_in, weight_mats, bias_rows, step_width):
    return lax.map(lambda packed: advance(packed[0], packed[1], packed[2], step_width), (states_in, weight_mats, bias_rows))


def through_block(initial, weight_mats, bias_rows, step_width):
    def layer_step(carry_state, layer_pair):
        next_state = advance(carry_state, layer_pair[0], layer_pair[1], step_width)
        return next_state, next_state
    return lax.scan(layer_step, initial, (weight_mats, bias_rows))


def reference(weights, biases, guesses):
    fine_width = 4.0 / (L_DEV * N_LAYER)
    block_width = L_DEV * fine_width
    group_width = GROUP * block_width
    layer_weights = weights.reshape(N_LAYER, L_DEV, D, D)
    layer_biases = biases.reshape(N_LAYER, L_DEV, D)
    head_weights = layer_weights[:, 0]
    head_biases = layer_biases[:, 0]
    fine_end = lax.map(lambda packed: through_block(packed[0], packed[1], packed[2], fine_width)[0], (guesses, layer_weights, layer_biases))
    coarse_head = advance_each(guesses, head_weights, head_biases, block_width)
    tau_one = jnp.concatenate([jnp.zeros_like(guesses[:1]), fine_end[:-1] - coarse_head[:-1]], axis=0)
    guess_parts = guesses.reshape(N_LAYER, BATCH // GROUP, GROUP, D)
    tau_parts = tau_one.reshape(N_LAYER, BATCH // GROUP, GROUP, D)
    phase_results = []
    for phase in range(GROUP):
        guess_rows = guess_parts[:, :, phase]
        tau_rows = tau_parts[:, :, phase]
        level = guess_rows[0]
        arrival = {}
        for block in range(1, N_LAYER):
            moved = advance(level, head_weights[block - 1], head_biases[block - 1], block_width) + tau_rows[block]
            if (block - phase) % GROUP == 0:
                arrival[block] = moved
                level = guess_rows[block]
            else:
                level = moved
        coarsest = {}
        if phase == 0:
            coarsest[0] = guess_rows[0]
        for block in range(1, N_LAYER):
            if (block - phase) % GROUP == 0:
                if block < GROUP:
                    coarsest[block] = arrival[block]
                else:
                    behind = advance(guess_rows[block - GROUP], head_weights[block - GROUP], head_biases[block - GROUP], group_width)
                    tau_two = arrival[block] - behind
                    coarsest[block] = advance(coarsest[block - GROUP], head_weights[block - GROUP], head_biases[block - GROUP], group_width) + tau_two
        value = guess_rows[0]
        column = [value]
        for block in range(1, N_LAYER):
            if (block - phase) % GROUP == 0:
                value = coarsest[block]
            else:
                value = advance(value, head_weights[block - 1], head_biases[block - 1], block_width) + tau_rows[block]
            column.append(value)
        phase_results.append(jnp.stack(column, axis=0))
    corrected = jnp.stack(phase_results, axis=2).reshape(N_LAYER, BATCH, D)
    states = lax.map(lambda packed: through_block(packed[0], packed[1], packed[2], fine_width)[1], (corrected, layer_weights, layer_biases))
    return states.reshape(LAYERS, BATCH, D).astype(jnp.bfloat16)
```

```python
import jax
import jax.numpy as jnp
from jax import lax
from jax.experimental import pallas as pl
from jax.experimental.pallas import tpu as pltpu
from jax.sharding import PartitionSpec as P

MESH = pl.DeviceIdType.MESH
GROUP = 4
NL = 32
NZ = 16
D = 512
ROWS = 512
PR = ROWS // GROUP
HR = PR // 2
KR = D // NZ
LD = 4
LANES = 128
FINE = 4.0 / 128
BLOCK = 4 * FINE
WIDE = 16 * FINE


def kernel(
    w_ref, b_ref, g_ref, o_ref,
    wf, natural, guess, tau, level_in, level_out, heads, hbias, arr, qg, taup,
    coarse_in, coarse_out, coarse, corr_other, first_out, first_in, hop_in, hop_out, fin,
    load_s, ring_s, ring_r, head_s, head_r, bias_s, bias_r, qg_s, qg_r, tau_s, tau_r, level_s, level_r,
    arr_s, arr_r, q_s, q_r, corr_s, corr_r, first_s, first_r, hop_s, hop_r,
):
    r = lax.axis_index("layer")
    z = lax.axis_index("dp")
    nxt = lax.rem(r + 1, NL)
    prv = lax.rem(r + NL - 1, NL)
    h = lax.rem(r // 4, 2)

    def flip(d):
        return d + 4 - 8 * lax.rem(d // 4, 2)

    mate = flip(r)
    x_next = lax.rem(r + 8, NL)
    x_prev = lax.rem(r + NL - 8, NL)
    mate_next = lax.rem(mate + 1, NL)
    next_mate = flip(nxt)
    hn = lax.rem(nxt // 4, 2)
    z_up = lax.rem(z + 1, NZ)
    z_dn = lax.rem(z + NZ - 1, NZ)

    def phase(back):
        return lax.rem(r - back + 2 * GROUP, GROUP)

    def to(layer, src, dst, send, recv):
        return pltpu.make_async_remote_copy(
            src_ref=src, dst_ref=dst, send_sem=send, recv_sem=recv,
            device_id=(layer, z), device_id_type=MESH)

    loads = [
        pltpu.make_async_copy(g_ref.at[0, :, pl.ds(c * LANES, LANES)], natural.at[c], load_s.at[c])
        for c in range(D // LANES)
    ]
    for load in loads:
        load.start()
    barrier = pltpu.get_barrier_semaphore()
    for dev in (
        (r, z_up), (r, z_dn), (nxt, z), (prv, z), (x_next, z), (x_prev, z), (mate, z),
        (mate_next, z), (flip(prv), z), (next_mate, z), (lax.rem(mate + NL - 1, NL), z),
    ):
        pl.semaphore_signal(barrier, inc=1, device_id=dev, device_id_type=MESH)

    mine = pl.ds(pl.multiple_of(z * KR, KR), KR)
    for layer in range(LD):
        wf[layer, mine, :] = w_ref[layer]
    pl.semaphore_wait(barrier, 11)

    def shard(layer, origin):
        o = lax.rem(origin + 2 * NZ, NZ)
        return wf.at[layer, pl.ds(pl.multiple_of(o * KR, KR), KR)]

    def ring(way, step, layer):
        origin = z - (step - 1) if way == 0 else z + (step - 1)
        part = shard(layer, origin)
        return pltpu.make_async_remote_copy(
            src_ref=part, dst_ref=part, send_sem=ring_s.at[way, step - 1, layer],
            recv_sem=ring_r.at[way, step - 1, layer],
            device_id=(r, z_up if way == 0 else z_dn), device_id_type=MESH)

    def ring_arrived(way, step, layer):
        origin = z - step if way == 0 else z + step
        part = shard(layer, origin)
        pltpu.make_async_remote_copy(
            src_ref=part, dst_ref=part, send_sem=ring_s.at[way, step - 1, layer],
            recv_sem=ring_r.at[way, step - 1, layer],
            device_id=(r, z_up if way == 0 else z_dn), device_id_type=MESH).wait_recv()

    def head_copy(origin, slot):
        o = lax.rem(origin + 2 * NZ, NZ)
        rows = pl.ds(pl.multiple_of(o * KR, KR), KR)
        return to(mate, wf.at[0, rows], heads.at[slot, rows], head_s.at[o], head_r.at[o])

    def last_step(way, layer):
        return (layer < 2) == (way == 0)

    for layer in range(LD):
        for way in range(2):
            ring(way, 1, layer).start()
    head_copy(z, h).start()
    bias_copy = to(mate, b_ref, hbias.at[h], bias_s.at[0], bias_r.at[0])
    bias_copy.start()
    hbias[h] = b_ref[...]
    for c in range(D // LANES):
        loads[c].wait()
        for p in range(GROUP):
            guess[p, :, pl.ds(c * LANES, LANES)] = natural[c, pl.ds(p, PR, stride=GROUP), :]

    def ring_body(step, carry):
        for layer in range(LD):
            for way in range(2):
                ring_arrived(way, step, layer)
                ring(way, step + 1, layer).start()
                if layer == 0:
                    head_copy(z - step if way == 0 else z + step, h).start()
        return carry

    lax.fori_loop(1, 7, ring_body, 0)
    for layer in range(LD):
        for way in range(2):
            ring_arrived(way, 7, layer)
            if last_step(way, layer):
                ring(way, 8, layer).start()
            if layer == 0:
                head_copy(z - 7 if way == 0 else z + 7, h).start()
    for layer in range(LD):
        for way in range(2):
            if last_step(way, layer):
                ring_arrived(way, 8, layer)
                if layer == 0:
                    head_copy(z - 8, h).start()

    def act(u, weight, bias):
        return jnp.tanh(jnp.dot(u.astype(jnp.bfloat16), weight, preferred_element_type=jnp.float32) + bias)

    def bias_row(layer):
        return b_ref[pl.ds(layer, 1), :]

    def half_rows(half):
        return pl.ds(pl.multiple_of(half * HR, HR), HR)

    def sweep(back):
        p = phase(back)
        start = guess[p]
        first = act(start, wf[0], bias_row(0))
        u = start + FINE * first
        for layer in range(1, LD):
            u = u + FINE * act(u, wf[layer], bias_row(layer))
        tau[p] = u - (start + BLOCK * first)
        return start, first, u

    def level_copy(m, c):
        rows = pl.ds(c * HR, HR)
        return to(nxt, level_out.at[m, rows], level_in.at[m, rows], level_s.at[m, c], level_r.at[m, c])

    start, first, end = sweep(0)
    level_out[0] = end
    for c in range(2):
        level_copy(0, c).start()
    level_out[4] = start + WIDE * first
    own_rows = half_rows(h)
    other_rows = half_rows(1 - h)
    qg[h] = level_out[4, own_rows, :]
    qg_copy = to(mate, level_out.at[4, other_rows], qg.at[h], qg_s.at[0], qg_r.at[0])
    qg_copy.start()
    taup[h] = tau[phase(0), own_rows, :]
    tau_copy = to(mate, tau.at[phase(0), other_rows], taup.at[h], tau_s.at[0], tau_r.at[0])
    tau_copy.start()
    own_head = pltpu.make_async_copy(wf.at[0], heads.at[h], bias_s.at[1])
    own_head.start()

    arr_near = to(nxt, level_out.at[3, half_rows(hn)], arr.at[hn], arr_s.at[0], arr_r.at[hn])
    arr_far = to(next_mate, level_out.at[3, half_rows(1 - hn)], arr.at[hn], arr_s.at[1], arr_r.at[hn])
    arr_start = to(mate, guess.at[0, pl.ds(HR, HR)], arr.at[0], arr_s.at[2], arr_r.at[0])

    @pl.when(r == 0)
    def _():
        arr_start.start()
        arr[0] = guess[0, pl.ds(0, HR), :]

    for m in range(1, 4):
        sweep(m)
        p = phase(m)
        for c in range(2):
            rows = pl.ds(c * HR, HR)
            level_copy(m - 1, c).wait_recv()
            u = jnp.where(r == 0, guess[p, rows, :], level_in[m - 1, rows, :])
            level_out[m, rows, :] = u + BLOCK * act(u, wf[0], bias_row(0)) + tau[p, rows, :]
            if m < 3:
                level_copy(m, c).start()
        if m == 3:
            @pl.when(r != NL - 1)
            def _():
                arr_near.start()
                arr_far.start()

    def wait_heads(o, carry):
        head_copy(o, h).wait_recv()
        return carry

    lax.fori_loop(0, NZ, wait_heads, 0)
    bias_copy.wait_recv()
    own_head.wait()
    qg_copy.wait_recv()
    tau_copy.wait_recv()

    def arrived(slot):
        to(nxt, level_out.at[3, pl.ds(0, HR)], arr.at[slot], arr_s.at[0], arr_r.at[slot]).wait_recv()

    @pl.when(jnp.logical_or(r != 0, h != 0))
    def _():
        arrived(0)

    arrived(1)
    x_pos = r // 8
    q_copy = to(x_next, coarse_out, coarse_in, q_s.at[0], q_r.at[0])

    @pl.when(x_pos == 0)
    def _():
        coarse[0] = arr[0]

    @pl.when(x_pos != 0)
    def _():
        q_copy.wait_recv()
        coarse[0] = arr[0] + coarse_in[...]

    ua = coarse[0]
    ta = act(ua, heads[0], hbias[0, pl.ds(0, 1), :])
    ub = arr[1] + ((ua + WIDE * ta) - qg[0])
    coarse[1] = ub
    tb = act(ub, heads[1], hbias[1, pl.ds(0, 1), :])

    @pl.when(x_pos != 3)
    def _():
        coarse_out[...] = (ub + WIDE * tb) - qg[1]
        q_copy.start()

    first_out[0] = ua + BLOCK * ta + taup[0]
    first_out[1] = ub + BLOCK * tb + taup[1]
    first_near = to(nxt, first_out.at[h], first_in.at[own_rows], first_s.at[0], first_r.at[h])
    first_far = to(mate_next, first_out.at[1 - h], first_in.at[own_rows], first_s.at[1], first_r.at[h])
    first_far.start()
    first_near.start()
    corr_copy = to(mate, coarse.at[1 - h], corr_other, corr_s.at[0], corr_r.at[0])
    corr_copy.start()

    def put(p, offset, count, values):
        for c in range(D // LANES):
            fin[c, pl.ds(p + GROUP * offset, count, stride=GROUP), :] = values[:, c * LANES:(c + 1) * LANES]

    put(phase(0), h * HR, HR, coarse[h])

    def hop(m, c):
        rows = pl.ds(c * HR, HR)
        return to(nxt, hop_out.at[m, rows], hop_in.at[m, rows], hop_s.at[m, c], hop_r.at[m, c])

    def first_arrived(half):
        to(nxt, first_out.at[0], first_in.at[half_rows(half)], first_s.at[0], first_r.at[half]).wait_recv()

    for m in range(1, 4):
        p = phase(m)
        for c in range(2):
            rows = pl.ds(c * HR, HR)
            if m == 1:
                first_arrived(c)
                got = first_in[rows, :]
            else:
                hop(m - 2, c).wait_recv()
                got = hop_in[m - 2, rows, :]
            u = jnp.where(r == 0, guess[p, rows, :], got)
            if m < 3:
                hop_out[m - 1, rows, :] = u + BLOCK * act(u, wf[0], bias_row(0)) + tau[p, rows, :]
                hop(m - 1, c).start()
            put(p, c * HR, HR, u)
    corr_copy.wait_recv()
    put(phase(0), (1 - h) * HR, HR, corr_other[...])

    for tile in range(4):
        rows = pl.ds(tile * 128, 128)
        u = jnp.concatenate([fin[c, rows, :] for c in range(D // LANES)], axis=1)
        for layer in range(LD):
            u = u + FINE * act(u, wf[layer], bias_row(layer))
            o_ref[layer, rows, :] = u.astype(jnp.bfloat16)

    def drain(step, carry):
        for layer in range(LD):
            for way in range(2):
                ring(way, step, layer).wait_send()
        return carry

    lax.fori_loop(1, 8, drain, 0)
    for layer in range(LD):
        for way in range(2):
            if last_step(way, layer):
                ring(way, 8, layer).wait_send()

    def drain_heads(o, carry):
        head_copy(o, h).wait_send()
        return carry

    lax.fori_loop(0, NZ, drain_heads, 0)
    bias_copy.wait_send()
    qg_copy.wait_send()
    tau_copy.wait_send()
    for m in range(3):
        for c in range(2):
            level_copy(m, c).wait_send()

    @pl.when(r == 0)
    def _():
        arr_start.wait_send()

    @pl.when(r != NL - 1)
    def _():
        arr_far.wait_send()
        arr_near.wait_send()

    @pl.when(x_pos != 3)
    def _():
        q_copy.wait_send()

    first_near.wait_send()
    first_far.wait_send()
    corr_copy.wait_send()
    for m in range(2):
        for c in range(2):
            hop(m, c).wait_send()


def per_device(weights, biases, guesses):
    f32, bf16 = jnp.float32, jnp.bfloat16
    dma = pltpu.SemaphoreType.DMA
    vmem = pl.BlockSpec(memory_space=pltpu.VMEM)
    scratch = [
        pltpu.VMEM((LD, D, D), bf16),
        pltpu.VMEM((D // LANES, ROWS, LANES), f32),
        pltpu.VMEM((GROUP, PR, D), f32),
        pltpu.VMEM((GROUP, PR, D), f32),
        pltpu.VMEM((3, PR, D), f32),
        pltpu.VMEM((5, PR, D), f32),
        pltpu.VMEM((2, D, D), bf16),
        pltpu.VMEM((2, LD, D), f32),
        pltpu.VMEM((2, HR, D), f32),
        pltpu.VMEM((2, HR, D), f32),
        pltpu.VMEM((2, HR, D), f32),
        pltpu.VMEM((HR, D), f32),
        pltpu.VMEM((HR, D), f32),
        pltpu.VMEM((2, HR, D), f32),
        pltpu.VMEM((HR, D), f32),
        pltpu.VMEM((2, HR, D), f32),
        pltpu.VMEM((PR, D), f32),
        pltpu.VMEM((2, PR, D), f32),
        pltpu.VMEM((2, PR, D), f32),
        pltpu.VMEM((D // LANES, ROWS, LANES), f32),
        dma((D // LANES,)),
        dma((2, 8, LD)), dma((2, 8, LD)),
        dma((NZ,)), dma((NZ,)),
        dma((2,)), dma((1,)),
        dma((1,)), dma((1,)),
        dma((1,)), dma((1,)),
        dma((3, 2)), dma((3, 2)),
        dma((3,)), dma((2,)),
        dma((1,)), dma((1,)),
        dma((1,)), dma((1,)),
        dma((2,)), dma((2,)),
        dma((2, 2)), dma((2, 2)),
    ]
    return pl.pallas_call(
        kernel,
        out_shape=jax.ShapeDtypeStruct((LD, ROWS, D), bf16),
        in_specs=[vmem, vmem, pl.BlockSpec(memory_space=pl.ANY)],
        out_specs=vmem,
        scratch_shapes=scratch,
        compiler_params=pltpu.CompilerParams(
            collective_id=1, has_side_effects=True, vmem_limit_bytes=48 * 2**20),
        cost_estimate=pl.CostEstimate(flops=3 * 10**9, bytes_accessed=3 * 2**20, transcendentals=3 * 10**6),
    )(weights, biases, guesses)


def solution(mesh):
    in_specs = (P("layer", "dp", None), P("layer", None), P("layer", "dp", None))
    out_specs = P("layer", "dp", None)
    return jax.shard_map(
        per_device, mesh=mesh, in_specs=in_specs, out_specs=out_specs, check_vma=False
    )
```

```python
import jax
import jax.numpy as jnp
from jax import lax
from jax.experimental import pallas as pl
from jax.experimental.pallas import tpu as pltpu
from jax.sharding import PartitionSpec as P

MESH = pl.DeviceIdType.MESH
GROUP = 4
QUAD = 4
NL = 32
NZ = 16
D = 512
LANES = 128
ROWS = 512
PR = ROWS // GROUP
HR = PR // 2
QR = PR // QUAD
KR = D // NZ
LD = 4
FINE = 4.0 / 128
BLOCK = 4 * FINE
WIDE = 16 * FINE


def kernel(
    w_ref, b_ref, g_ref, o_ref,
    wf, bias, natural, guess, base_in, tau, inc_in, inc_out, heads, hbias, part, part_act, arr, base_far,
    coarse_in, coarse_out, coarse, corr_in, first_out, first_in, hop_in, hop_out, fin,
    load_s, ring_s, ring_r, head_s, head_r, bias_s, bias_r, part_s, part_r, base_s, base_r, far_s, far_r,
    level_s, level_r, arr_s, arr_r, q_s, q_r, corr_s, corr_r, first_s, first_r, hop_s, hop_r, own_s,
):
    r = lax.axis_index("layer")
    z = lax.axis_index("dp")
    nxt = lax.rem(r + 1, NL)
    prv = lax.rem(r + NL - 1, NL)
    spot = lax.rem(r // 4, QUAD)
    spot_next = lax.rem(nxt // 4, QUAD)
    far = lax.rem(r + 16, NL)
    z_up = lax.rem(z + 1, NZ)
    z_dn = lax.rem(z + NZ - 1, NZ)
    first_half = r < 16
    starts = jnp.logical_and(first_half, lax.rem(r, GROUP) == 0)
    starts_later = jnp.logical_and(first_half, lax.rem(r, GROUP) != 0)

    def phase(back):
        return lax.rem(r - back + 2 * GROUP, GROUP)

    def to(layer, src, dst, send, recv):
        return pltpu.make_async_remote_copy(
            src_ref=src, dst_ref=dst, send_sem=send, recv_sem=recv,
            device_id=(layer, z), device_id_type=MESH)

    loads = [
        pltpu.make_async_copy(
            w_ref.at[layer], wf.at[layer, pl.ds(pl.multiple_of(z * KR, KR), KR)], load_s.at[layer])
        for layer in range(LD)
    ]
    loads.append(pltpu.make_async_copy(b_ref, bias, load_s.at[LD]))
    guess_loads = [
        pltpu.make_async_copy(g_ref.at[0, :, pl.ds(c * LANES, LANES)], natural.at[c], load_s.at[LD + 1 + c])
        for c in range(D // LANES)
    ]
    for load in loads + guess_loads:
        load.start()

    def peer(d, i):
        j = lax.rem(d // 4, QUAD)
        other = j + 1 - 2 * lax.rem(j, 2) if i == 1 else lax.rem(j + 2, 4) if i == 2 else 3 - j
        return d + 4 * (other - j)

    barrier = pltpu.get_barrier_semaphore()
    greeted = [(r, z_up), (r, z_dn), (nxt, z), (prv, z), (far, z)]
    for i in range(1, QUAD):
        greeted += [
            (peer(r, i), z),
            (lax.rem(peer(r, i) + 1, NL), z), (peer(prv, i), z),
            (peer(nxt, i), z), (lax.rem(peer(r, i) + NL - 1, NL), z),
        ]
    for dev in greeted:
        pl.semaphore_signal(barrier, inc=1, device_id=dev, device_id_type=MESH)
    for load in loads:
        load.wait()
    pl.semaphore_wait(barrier, len(greeted))

    def shard(layer, origin):
        o = lax.rem(origin + 2 * NZ, NZ)
        return wf.at[layer, pl.ds(pl.multiple_of(o * KR, KR), KR)]

    def ring(way, step, layer, arrived=False):
        back = step if arrived else step - 1
        block = shard(layer, z - back if way == 0 else z + back)
        return pltpu.make_async_remote_copy(
            src_ref=block, dst_ref=block, send_sem=ring_s.at[way, step - 1, layer],
            recv_sem=ring_r.at[way, step - 1, layer],
            device_id=(r, z_up if way == 0 else z_dn), device_id_type=MESH)

    def owner(s):
        return r + 4 * (s - spot)

    def each_peer(action):
        for s in range(QUAD):
            @pl.when(s != spot)
            def _():
                action(s)

    def head_copy(s, slot, origin):
        o = lax.rem(origin + 2 * NZ, NZ)
        rows = pl.ds(pl.multiple_of(o * KR, KR), KR)
        return to(owner(s), wf.at[0, rows], heads.at[slot, rows], head_s.at[s, o], head_r.at[slot, o])

    mate = spot + 1 - 2 * lax.rem(spot, 2)
    across = lax.rem(spot + 2, QUAD)
    diagonal = 3 - spot

    def send_head(origin):
        head_copy(mate, spot, origin).start()
        head_copy(across, spot, origin).start()

    def head_hand_on(origin):
        o = lax.rem(origin + 2 * NZ, NZ)
        rows = pl.ds(pl.multiple_of(o * KR, KR), KR)
        return to(
            owner(across), heads.at[mate, rows], heads.at[mate, rows], head_s.at[diagonal, o], head_r.at[mate, o])

    def hand_on(origin):
        head_copy(mate, mate, origin).wait_recv()
        head_hand_on(origin).start()

    def bias_copy(s, slot):
        return to(owner(s), bias, hbias.at[slot], bias_s.at[s], bias_r.at[slot])

    def quarter(j):
        if not isinstance(j, int):
            return pl.ds(pl.multiple_of(j * QR, QR), QR)
        return pl.ds(j * QR, QR)

    def part_copy(s, slot):
        return to(owner(s), guess.at[phase(0), quarter(s)], part.at[slot], part_s.at[s], part_r.at[slot])

    def base_copy(m):
        src = guess.at[phase(0)] if m == 0 else base_in.at[m - 1]
        return to(nxt, src, base_in.at[m], base_s.at[m], base_r.at[m])

    def last_step(way, layer):
        return (layer < 2) == (way == 0)

    for layer in range(LD):
        for way in range(2):
            ring(way, 1, layer).start()
    send_head(z)
    each_peer(lambda s: bias_copy(s, spot).start())
    for c in range(D // LANES):
        guess_loads[c].wait()
        for p in range(GROUP):
            guess[p, :, pl.ds(c * LANES, LANES)] = natural[c, pl.ds(p, PR, stride=GROUP), :]

    @pl.when(r != NL - 1)
    def _():
        base_copy(0).start()

    each_peer(lambda s: part_copy(s, spot).start())
    part[spot] = guess[phase(0), quarter(spot), :]
    hbias[spot] = bias[...]

    @pl.when(r == 0)
    def _():
        for m in range(1, 4):
            base_in[m - 1] = guess[phase(m)]
            inc_in[m - 1] = jnp.zeros((PR, D), jnp.bfloat16)
        first_in[...] = guess[phase(1)]
        hop_in[0] = guess[phase(2)]
        hop_in[1] = guess[phase(3)]

    def ring_body(step, carry):
        for layer in range(LD):
            for way in range(2):
                ring(way, step, layer, True).wait_recv()
                ring(way, step + 1, layer).start()
                if layer == 0:
                    send_head(z - step if way == 0 else z + step)
        return carry

    def ring_and_hand_on(step, carry):
        ring_body(step, carry)
        hand_on(z - step + 2)
        hand_on(z + step - 2)
        return carry

    def far_copy(s):
        return to(nxt + 4 * s, base_in.at[2, quarter(s)], base_far, far_s.at[s], far_r.at[0])

    for m in range(3):
        lax.fori_loop(1 + 2 * m, 3 + 2 * m, ring_body if m == 0 else ring_and_hand_on, 0)
        if m == 0:
            hand_on(z)

        @pl.when(r != 0)
        def _():
            base_copy(m).wait_recv()

        if m < 2:
            @pl.when(r != NL - 1)
            def _():
                base_copy(m + 1).start()
        else:
            @pl.when(r < GROUP - 1)
            def _():
                for s in range(QUAD):
                    far_copy(s).start()

    for layer in range(LD):
        for way in range(2):
            ring(way, 7, layer, True).wait_recv()
            if last_step(way, layer):
                ring(way, 8, layer).start()
            if layer == 0:
                send_head(z - 7 if way == 0 else z + 7)

    hand_on(z - 5)
    hand_on(z + 5)

    def finish(layer):
        way = 0 if layer < 2 else 1
        ring(way, 8, layer, True).wait_recv()

    def act(u, weight, row):
        return jnp.tanh(jnp.dot(u.astype(jnp.bfloat16), weight, preferred_element_type=jnp.float32) + row)

    def bias_row(layer):
        return bias[pl.ds(layer, 1), :]

    finish(0)
    send_head(z - 8)
    own_head = pltpu.make_async_copy(wf.at[0], heads.at[spot], own_s.at[0])
    own_head.start()
    hand_on(z - 6)
    hand_on(z + 6)
    for back in range(GROUP):
        tau[phase(back)] = act(guess[phase(back)], wf[0], bias_row(0))

    def sweep(back, first_time=False):
        p = phase(back)
        start, first = guess[p], tau[p]
        inc = FINE * first
        for layer in range(1, LD):
            if first_time:
                finish(layer)
            inc = inc + FINE * act(start + inc, wf[layer], bias_row(layer))
        tau[p] = inc - BLOCK * first
        return inc

    def chunk(c):
        return pl.ds(c * HR, HR)

    def level_copy(m, c):
        return to(nxt, inc_out.at[m, chunk(c)], inc_in.at[m, chunk(c)], level_s.at[m, c], level_r.at[m, c])

    inc_out[0] = sweep(0, True).astype(jnp.bfloat16)

    @pl.when(r != NL - 1)
    def _():
        for c in range(2):
            level_copy(0, c).start()

    hand_on(z - 7)
    hand_on(z + 7)
    hand_on(z - 8)

    def arr_copy(s):
        return to(
            nxt + 4 * (s - spot_next), inc_out.at[3, quarter(s)], arr.at[spot_next], arr_s.at[s], arr_r.at[spot_next])

    for m in range(1, 4):
        sweep(m)
        p = phase(m)
        for c in range(2):
            @pl.when(r != 0)
            def _():
                level_copy(m - 1, c).wait_recv()

            before = inc_in[m - 1, chunk(c), :].astype(jnp.float32)
            u = base_in[m - 1, chunk(c), :] + before
            after = before + BLOCK * act(u, wf[0], bias_row(0)) + tau[p, chunk(c), :]
            inc_out[m, chunk(c), :] = after.astype(jnp.bfloat16)

            @pl.when(r != NL - 1)
            def _():
                if m < 3:
                    level_copy(m, c).start()
                else:
                    arr_copy(2 * c).start()
                    arr_copy(2 * c + 1).start()

    own_head.wait()

    def wait_from(s):
        def wait_head(o, carry):
            head_copy(s, s, o).wait_recv()
            return carry

        @pl.when(s != mate)
        def _():
            lax.fori_loop(0, NZ, wait_head, 0)

        bias_copy(s, s).wait_recv()
        part_copy(s, s).wait_recv()

    each_peer(wait_from)
    for s in range(QUAD):
        part_act[s] = act(part[s], heads[s], hbias[s, pl.ds(0, 1), :])

    def arrived(s):
        to(nxt, inc_out.at[3, quarter(s)], arr.at[s], arr_s.at[s], arr_r.at[s]).wait_recv()

    q_copy = to(far, coarse_out, coarse_in, q_s.at[0], q_r.at[0])

    @pl.when(starts)
    def _():
        coarse[0] = part[0]

    @pl.when(starts_later)
    def _():
        far_copy(0).wait_recv()
        arrived(0)
        coarse[0] = base_far[...] + arr[0].astype(jnp.float32)

    @pl.when(jnp.logical_not(first_half))
    def _():
        arrived(0)

    for s in range(1, QUAD):
        arrived(s)

    @pl.when(jnp.logical_not(first_half))
    def _():
        q_copy.wait_recv()
        coarse[0] = coarse_in[...] + arr[0].astype(jnp.float32)

    def first_copy(s, place):
        return to(
            lax.rem(owner(s) + 1, NL), first_out.at[s], first_in.at[quarter(place)], first_s.at[s], first_r.at[place])

    def corr_copy(s, place):
        return to(owner(s), coarse.at[s], corr_in.at[quarter(place)], corr_s.at[s], corr_r.at[place])

    u = coarse[0]
    for s in range(QUAD):
        change = act(u, heads[s], hbias[s, pl.ds(0, 1), :]) - part_act[s]
        following = u + WIDE * change
        if s == QUAD - 1:
            @pl.when(first_half)
            def _():
                coarse_out[...] = following
                q_copy.start()

        first_out[s] = u + BLOCK * change

        @pl.when(owner(s) != NL - 1)
        def _():
            first_copy(s, spot).start()

        @pl.when(s != spot)
        def _():
            corr_copy(s, spot).start()

        if s < QUAD - 1:
            u = following + arr[s + 1].astype(jnp.float32)
            coarse[s + 1] = u

    def put(p, offset, count, values):
        for c in range(D // LANES):
            fin[c, pl.ds(p + GROUP * offset, count, stride=GROUP), :] = values[:, c * LANES:(c + 1) * LANES]

    put(phase(0), spot * QR, QR, coarse[spot])

    def hop(m, c):
        return to(nxt, hop_out.at[m, chunk(c)], hop_in.at[m, chunk(c)], hop_s.at[m, c], hop_r.at[m, c])

    for m in range(1, 4):
        p = phase(m)
        for c in range(2):
            @pl.when(r != 0)
            def _():
                if m == 1:
                    first_copy(0, 2 * c).wait_recv()
                    first_copy(0, 2 * c + 1).wait_recv()
                else:
                    hop(m - 2, c).wait_recv()

            if m == 1:
                u = first_in[chunk(c), :] + inc_in[0, chunk(c), :].astype(jnp.float32)
            else:
                u = hop_in[m - 2, chunk(c), :]
            if m < 3:
                hop_out[m - 1, chunk(c), :] = u + BLOCK * act(u, wf[0], bias_row(0)) + tau[p, chunk(c), :]

                @pl.when(r != NL - 1)
                def _():
                    hop(m - 1, c).start()

            put(p, c * HR, HR, u)

    def take_corr(s):
        corr_copy(s, s).wait_recv()
        put(phase(0), s * QR, QR, corr_in[quarter(s), :])

    each_peer(take_corr)

    for tile in range(4):
        rows = pl.ds(tile * 128, 128)
        u = jnp.concatenate([fin[c, rows, :] for c in range(D // LANES)], axis=1)
        for layer in range(LD):
            u = u + FINE * act(u, wf[layer], bias_row(layer))
            o_ref[layer, rows, :] = u.astype(jnp.bfloat16)

    def drain(step, carry):
        for layer in range(LD):
            for way in range(2):
                ring(way, step, layer).wait_send()
        return carry

    lax.fori_loop(1, 8, drain, 0)
    for layer in range(LD):
        for way in range(2):
            if last_step(way, layer):
                ring(way, 8, layer).wait_send()

    def drain_peer(s):
        def drain_head(o, carry):
            head_copy(s, spot, o).wait_send()
            return carry

        lax.fori_loop(0, NZ, drain_head, 0)
        bias_copy(s, spot).wait_send()
        part_copy(s, spot).wait_send()
        corr_copy(s, spot).wait_send()

    each_peer(drain_peer)

    @pl.when(r != NL - 1)
    def _():
        for m in range(3):
            base_copy(m).wait_send()
            for c in range(2):
                level_copy(m, c).wait_send()
        for s in range(QUAD):
            arr_copy(s).wait_send()
        for m in range(2):
            for c in range(2):
                hop(m, c).wait_send()

    @pl.when(r < GROUP - 1)
    def _():
        for s in range(QUAD):
            far_copy(s).wait_send()

    @pl.when(first_half)
    def _():
        q_copy.wait_send()

    for s in range(QUAD):
        @pl.when(owner(s) != NL - 1)
        def _():
            first_copy(s, spot).wait_send()


def per_device(weights, biases, guesses):
    f32, bf16 = jnp.float32, jnp.bfloat16
    dma = pltpu.SemaphoreType.DMA
    hbm = pl.BlockSpec(memory_space=pltpu.HBM)
    scratch = dict(
        wf=pltpu.VMEM((LD, D, D), bf16),
        bias=pltpu.VMEM((LD, D), f32),
        natural=pltpu.VMEM((D // LANES, ROWS, LANES), f32),
        guess=pltpu.VMEM((GROUP, PR, D), f32),
        base_in=pltpu.VMEM((3, PR, D), f32),
        tau=pltpu.VMEM((GROUP, PR, D), f32),
        inc_in=pltpu.VMEM((3, PR, D), bf16),
        inc_out=pltpu.VMEM((4, PR, D), bf16),
        heads=pltpu.VMEM((QUAD, D, D), bf16),
        hbias=pltpu.VMEM((QUAD, LD, D), f32),
        part=pltpu.VMEM((QUAD, QR, D), f32),
        part_act=pltpu.VMEM((QUAD, QR, D), f32),
        arr=pltpu.VMEM((QUAD, QR, D), bf16),
        base_far=pltpu.VMEM((QR, D), f32),
        coarse_in=pltpu.VMEM((QR, D), f32),
        coarse_out=pltpu.VMEM((QR, D), f32),
        coarse=pltpu.VMEM((QUAD, QR, D), f32),
        corr_in=pltpu.VMEM((PR, D), f32),
        first_out=pltpu.VMEM((QUAD, QR, D), f32),
        first_in=pltpu.VMEM((PR, D), f32),
        hop_in=pltpu.VMEM((2, PR, D), f32),
        hop_out=pltpu.VMEM((2, PR, D), f32),
        fin=pltpu.VMEM((D // LANES, ROWS, LANES), f32),
        load_s=dma((LD + 1 + D // LANES,)),
        ring_s=dma((2, 8, LD)), ring_r=dma((2, 8, LD)),
        head_s=dma((QUAD, NZ)), head_r=dma((QUAD, NZ)),
        bias_s=dma((QUAD,)), bias_r=dma((QUAD,)),
        part_s=dma((QUAD,)), part_r=dma((QUAD,)),
        base_s=dma((3,)), base_r=dma((3,)),
        far_s=dma((QUAD,)), far_r=dma((1,)),
        level_s=dma((3, 2)), level_r=dma((3, 2)),
        arr_s=dma((QUAD,)), arr_r=dma((QUAD,)),
        q_s=dma((1,)), q_r=dma((1,)),
        corr_s=dma((QUAD,)), corr_r=dma((QUAD,)),
        first_s=dma((QUAD,)), first_r=dma((QUAD,)),
        hop_s=dma((2, 2)), hop_r=dma((2, 2)),
        own_s=dma((1,)),
    )
    return pl.pallas_call(
        kernel,
        out_shape=jax.ShapeDtypeStruct((LD, ROWS, D), bf16),
        in_specs=[hbm, hbm, hbm],
        out_specs=pl.BlockSpec(memory_space=pltpu.VMEM),
        scratch_shapes=scratch,
        compiler_params=pltpu.CompilerParams(
            collective_id=1, has_side_effects=True, vmem_limit_bytes=40 * 2**20),
        cost_estimate=pl.CostEstimate(flops=3 * 10**9, bytes_accessed=3 * 2**20, transcendentals=3 * 10**6),
    )(weights, biases, guesses)


def solution(mesh):
    in_specs = (P("layer", "dp", None), P("layer", None), P("layer", "dp", None))
    out_specs = P("layer", "dp", None)
    return jax.shard_map(
        per_device, mesh=mesh, in_specs=in_specs, out_specs=out_specs, check_vma=False
    )
```

```python
import jax
import jax.numpy as jnp
from jax import lax
from jax.experimental import pallas as pl
from jax.experimental.pallas import tpu as pltpu
from jax.sharding import PartitionSpec as P

MESH = pl.DeviceIdType.MESH
GROUP = 4
QUAD = 4
NL = 32
NZ = 16
D = 512
LANES = 128
ROWS = 512
PR = ROWS // GROUP
HR = PR // 2
QR = PR // QUAD
KR = D // NZ
LD = 4
FINE = 4.0 / 128
BLOCK = 4 * FINE
WIDE = 16 * FINE


def kernel(
    w_ref, b_ref, g_ref, o_ref,
    wf, bias, natural, guess, base_in, tau, inc_in, inc_out, heads, hbias, part, part_act, arr, base_far,
    coarse_in, coarse_out, coarse, corr_in, first_out, first_in, hop_in, hop_out, fin, first_now,
    load_s, ring_s, ring_r, head_s, head_r, bias_s, bias_r, part_s, part_r, base_s, base_r, far_s, far_r,
    level_s, level_r, arr_s, arr_r, q_s, q_r, corr_s, corr_r, first_s, first_r, hop_s, hop_r, own_s, done, out_s,
):
    r = lax.axis_index("layer")
    z = lax.axis_index("dp")
    nxt = lax.rem(r + 1, NL)
    prv = lax.rem(r + NL - 1, NL)
    spot = lax.rem(r // 4, QUAD)
    spot_next = lax.rem(nxt // 4, QUAD)
    far = lax.rem(r + 16, NL)
    first_half = r < 16
    starts = jnp.logical_and(first_half, lax.rem(r, GROUP) == 0)
    starts_later = jnp.logical_and(first_half, lax.rem(r, GROUP) != 0)

    def phase(back):
        return lax.rem(r - back + 2 * GROUP, GROUP)

    def to(layer, src, dst, send, recv):
        return pltpu.make_async_remote_copy(
            src_ref=src, dst_ref=dst, send_sem=send, recv_sem=recv,
            device_id=(layer, z), device_id_type=MESH)

    loads = [
        pltpu.make_async_copy(
            w_ref.at[layer], wf.at[layer, pl.ds(pl.multiple_of(z * KR, KR), KR)], load_s.at[layer])
        for layer in range(LD)
    ]
    loads.append(pltpu.make_async_copy(b_ref, bias, load_s.at[LD]))
    guess_loads = [
        pltpu.make_async_copy(g_ref.at[0, :, pl.ds(c * LANES, LANES)], natural.at[c], load_s.at[LD + 1 + c])
        for c in range(D // LANES)
    ]
    for load in loads + guess_loads:
        load.start()

    def peer(d, i):
        j = lax.rem(d // 4, QUAD)
        other = j + 1 - 2 * lax.rem(j, 2) if i == 1 else lax.rem(j + 2, 4) if i == 2 else 3 - j
        return d + 4 * (other - j)

    barrier = pltpu.get_barrier_semaphore()
    greeted = [(r, lax.rem(z + d, NZ)) for d in (1, NZ - 1)]
    greeted += [(nxt, z), (prv, z), (far, z)]
    for i in range(1, QUAD):
        greeted += [
            (peer(r, i), z),
            (lax.rem(peer(r, i) + 1, NL), z), (peer(prv, i), z),
            (peer(nxt, i), z), (lax.rem(peer(r, i) + NL - 1, NL), z),
        ]
    for dev in greeted:
        pl.semaphore_signal(barrier, inc=1, device_id=dev, device_id_type=MESH)
    for load in loads:
        load.wait()
    pl.semaphore_wait(barrier, len(greeted))

    def shard(layer, origin):
        o = lax.rem(origin + 2 * NZ, NZ)
        return wf.at[layer, pl.ds(pl.multiple_of(o * KR, KR), KR)]

    def ring(way, step, layer, arrived=False):
        back = step if arrived else step - 1
        block = shard(layer, z - back if way == 0 else z + back)
        return pltpu.make_async_remote_copy(
            src_ref=block, dst_ref=block, send_sem=ring_s.at[way, step - 1, layer],
            recv_sem=ring_r.at[way, step - 1, layer],
            device_id=(r, lax.rem(z + (1 if way == 0 else NZ - 1), NZ)), device_id_type=MESH)

    def owner(s):
        return r + 4 * (s - spot)

    def each_peer(action):
        for s in range(QUAD):
            @pl.when(s != spot)
            def _():
                action(s)

    def head_copy(s, slot, origin):
        o = lax.rem(origin + 2 * NZ, NZ)
        rows = pl.ds(pl.multiple_of(o * KR, KR), KR)
        return to(owner(s), wf.at[0, rows], heads.at[slot, rows], head_s.at[s, o], head_r.at[slot, o])

    mate = spot + 1 - 2 * lax.rem(spot, 2)
    across = lax.rem(spot + 2, QUAD)
    diagonal = 3 - spot

    def send_head(origin):
        head_copy(mate, spot, origin).start()
        head_copy(across, spot, origin).start()

    def head_hand_on(origin):
        o = lax.rem(origin + 2 * NZ, NZ)
        rows = pl.ds(pl.multiple_of(o * KR, KR), KR)
        return to(
            owner(across), heads.at[mate, rows], heads.at[mate, rows], head_s.at[diagonal, o], head_r.at[mate, o])

    def hand_on(origin):
        head_copy(mate, mate, origin).wait_recv()
        head_hand_on(origin).start()

    def bias_copy(s, slot):
        return to(owner(s), bias, hbias.at[slot], bias_s.at[s], bias_r.at[slot])

    def quarter(j):
        if not isinstance(j, int):
            return pl.ds(pl.multiple_of(j * QR, QR), QR)
        return pl.ds(j * QR, QR)

    def part_copy(s, slot):
        return to(owner(s), guess.at[phase(0), quarter(s)], part.at[slot], part_s.at[s], part_r.at[slot])

    def base_copy(m):
        src = guess.at[phase(0)] if m == 0 else base_in.at[m - 1]
        return to(nxt, src, base_in.at[m], base_s.at[m], base_r.at[m])

    def last_step(way, layer):
        return (layer < 2) == (way == 0)

    for layer in range(LD):
        for way in range(2):
            ring(way, 1, layer).start()
    send_head(z)
    each_peer(lambda s: bias_copy(s, spot).start())
    for c in range(D // LANES):
        guess_loads[c].wait()
        for p in range(GROUP):
            guess[p, :, pl.ds(c * LANES, LANES)] = natural[c, pl.ds(p, PR, stride=GROUP), :]

    @pl.when(r != NL - 1)
    def _():
        base_copy(0).start()

    each_peer(lambda s: part_copy(s, spot).start())
    part[spot] = guess[phase(0), quarter(spot), :]
    hbias[spot] = bias[...]

    @pl.when(r == 0)
    def _():
        for m in range(1, 4):
            base_in[m - 1] = guess[phase(m)]
            inc_in[m - 1] = jnp.zeros((PR, D), jnp.bfloat16)
        first_in[...] = guess[phase(1)]
        hop_in[0] = guess[phase(2)]
        hop_in[1] = guess[phase(3)]

    def ring_body(step, carry):
        for layer in range(LD):
            for way in range(2):
                ring(way, step, layer, True).wait_recv()
                ring(way, step + 1, layer).start()
                if layer == 0:
                    send_head(z - step if way == 0 else z + step)
        return carry

    def ring_and_hand_on(step, carry):
        ring_body(step, carry)
        hand_on(z - step + 3)

        @pl.when(step > 3)
        def _():
            hand_on(z + step - 3)

        return carry

    def far_copy(s):
        return to(nxt + 4 * s, base_in.at[2, quarter(s)], base_far, far_s.at[s], far_r.at[0])

    for m in range(3):
        lax.fori_loop(1 + 2 * m, 3 + 2 * m, ring_body if m == 0 else ring_and_hand_on, 0)

        @pl.when(r != 0)
        def _():
            base_copy(m).wait_recv()

        if m < 2:
            @pl.when(r != NL - 1)
            def _():
                base_copy(m + 1).start()
        else:
            @pl.when(r < GROUP - 1)
            def _():
                for s in range(QUAD):
                    far_copy(s).start()

    for layer in range(LD):
        for way in range(2):
            ring(way, 7, layer, True).wait_recv()
            if last_step(way, layer):
                ring(way, 8, layer).start()
            if layer == 0:
                send_head(z - 7 if way == 0 else z + 7)

    hand_on(z - 4)
    hand_on(z + 4)

    def finish(layer):
        way = 0 if layer < 2 else 1
        ring(way, 8, layer, True).wait_recv()

    def act(u, weight, row):
        return jnp.tanh(jnp.dot(u.astype(jnp.bfloat16), weight, preferred_element_type=jnp.float32) + row)

    def bias_row(layer):
        return bias[pl.ds(layer, 1), :]

    finish(0)
    send_head(z - 8)
    own_head = pltpu.make_async_copy(wf.at[0], heads.at[spot], own_s.at[0])
    own_head.start()

    def sweep(back, first_time=False):
        p = phase(back)
        start = guess[p]
        first = act(start, wf[0], bias_row(0))
        inc = FINE * first
        for layer in range(1, LD):
            if first_time:
                finish(layer)
            inc = inc + FINE * act(start + inc, wf[layer], bias_row(layer))
        tau[p] = inc - BLOCK * first
        return inc

    def chunk(c):
        return pl.ds(c * HR, HR)

    def level_copy(m, c):
        return to(nxt, inc_out.at[m, chunk(c)], inc_in.at[m, chunk(c)], level_s.at[m, c], level_r.at[m, c])

    inc_out[0] = sweep(0, True).astype(jnp.bfloat16)

    @pl.when(r != NL - 1)
    def _():
        for c in range(2):
            level_copy(0, c).start()


    def arr_copy(s):
        return to(
            nxt + 4 * (s - spot_next), inc_out.at[3, quarter(s)], arr.at[spot_next], arr_s.at[s], arr_r.at[spot_next])

    for m in range(1, 4):
        sweep(m)
        p = phase(m)
        for c in range(2):
            @pl.when(r != 0)
            def _():
                level_copy(m - 1, c).wait_recv()

            before = inc_in[m - 1, chunk(c), :].astype(jnp.float32)
            u = base_in[m - 1, chunk(c), :] + before
            after = before + BLOCK * act(u, wf[0], bias_row(0)) + tau[p, chunk(c), :]
            inc_out[m, chunk(c), :] = after.astype(jnp.bfloat16)

            @pl.when(r != NL - 1)
            def _():
                if m < 3:
                    level_copy(m, c).start()
                else:
                    arr_copy(2 * c).start()
                    arr_copy(2 * c + 1).start()

        if m == 1:
            for back in (5, 6):
                hand_on(z - back)
                hand_on(z + back)
        elif m == 2:
            hand_on(z - 7)
            hand_on(z + 7)
            hand_on(z - 8)

    own_head.wait()

    def wait_from(s):
        def wait_head(o, carry):
            head_copy(s, s, o).wait_recv()
            return carry

        @pl.when(s != mate)
        def _():
            lax.fori_loop(0, NZ, wait_head, 0)

        bias_copy(s, s).wait_recv()
        part_copy(s, s).wait_recv()

    each_peer(wait_from)
    for s in range(QUAD):
        part_act[s] = act(part[s], heads[s], hbias[s, pl.ds(0, 1), :])

    def arrived(s):
        to(nxt, inc_out.at[3, quarter(s)], arr.at[s], arr_s.at[s], arr_r.at[s]).wait_recv()

    q_copy = to(far, coarse_out, coarse_in, q_s.at[0], q_r.at[0])

    @pl.when(starts)
    def _():
        coarse[0] = part[0]

    @pl.when(starts_later)
    def _():
        far_copy(0).wait_recv()
        arrived(0)
        coarse[0] = base_far[...] + arr[0].astype(jnp.float32)

    @pl.when(jnp.logical_not(first_half))
    def _():
        arrived(0)

    for s in range(1, QUAD):
        arrived(s)

    @pl.when(jnp.logical_not(first_half))
    def _():
        q_copy.wait_recv()
        coarse[0] = coarse_in[...] + arr[0].astype(jnp.float32)

    def first_copy(s, place):
        return to(
            lax.rem(owner(s) + 1, NL), first_out.at[s], first_in.at[quarter(place)], first_s.at[s], first_r.at[place])

    def corr_copy(s, place):
        return to(owner(s), coarse.at[s], corr_in.at[quarter(place)], corr_s.at[s], corr_r.at[place])

    u = coarse[0]
    for s in range(QUAD):
        change = act(u, heads[s], hbias[s, pl.ds(0, 1), :]) - part_act[s]
        following = u + WIDE * change
        if s == QUAD - 1:
            @pl.when(first_half)
            def _():
                coarse_out[...] = following
                q_copy.start()

        first_out[s] = u + BLOCK * change

        @pl.when(jnp.logical_and(jnp.logical_not(first_half), owner(s) != NL - 1))
        def _():
            first_copy(s, spot).start()

        if s < QUAD - 1:
            u = following + arr[s + 1].astype(jnp.float32)
            coarse[s + 1] = u

    for s in range(QUAD):
        @pl.when(first_half)
        def _():
            first_copy(s, spot).start()

    each_peer(lambda s: corr_copy(s, spot).start())

    def put(layer, p, values):
        for c in range(D // LANES):
            fin[layer, c, pl.ds(p, PR, stride=GROUP), :] = values[:, c * LANES:(c + 1) * LANES]

    def settle(back, u):
        for layer in range(LD):
            u = u + FINE * act(u, wf[layer], bias_row(layer))
            put(layer, phase(back), u)

    corr_in[quarter(spot), :] = coarse[spot]

    def hop(m, c):
        return to(nxt, hop_out.at[m, quarter(c)], hop_in.at[m, quarter(c)], hop_s.at[m, c], hop_r.at[m, c])

    for m in range(1, 4):
        p = phase(m)
        for c in range(QUAD):
            @pl.when(r != 0)
            def _():
                if m == 1:
                    first_copy(0, c).wait_recv()
                else:
                    hop(m - 2, c).wait_recv()

            if m == 1:
                u = first_in[quarter(c), :] + inc_in[0, quarter(c), :].astype(jnp.float32)
                first_now[quarter(c), :] = u
            elif m == 2:
                u = hop_in[0, quarter(c), :]
            if m < 3:
                hop_out[m - 1, quarter(c), :] = u + BLOCK * act(u, wf[0], bias_row(0)) + tau[p, quarter(c), :]

                @pl.when(r != NL - 1)
                def _():
                    hop(m - 1, c).start()

        if m == 1:
            settle(1, first_now[...])
        else:
            settle(m, hop_in[m - 2])
        if m == 2:
            each_peer(lambda s: corr_copy(s, s).wait_recv())
            settle(0, corr_in[...])

    def out_copy(tile, layer):
        rows = pl.ds(tile * 128, 128)
        return pltpu.make_async_copy(done.at[layer, rows], o_ref.at[layer, rows], out_s.at[tile, layer])

    for layer in range(LD):
        for tile in range(4):
            rows = pl.ds(tile * 128, 128)
            for c in range(D // LANES):
                done[layer, rows, pl.ds(c * LANES, LANES)] = fin[layer, c, rows, :].astype(jnp.bfloat16)
            out_copy(tile, layer).start()

    def drain(step, carry):
        for layer in range(LD):
            for way in range(2):
                ring(way, step, layer).wait_send()
        return carry

    lax.fori_loop(1, 8, drain, 0)
    for layer in range(LD):
        for way in range(2):
            if last_step(way, layer):
                ring(way, 8, layer).wait_send()

    def drain_peer(s):
        def drain_head(o, carry):
            head_copy(s, spot, o).wait_send()
            return carry

        lax.fori_loop(0, NZ, drain_head, 0)
        bias_copy(s, spot).wait_send()
        part_copy(s, spot).wait_send()
        corr_copy(s, spot).wait_send()

    each_peer(drain_peer)

    @pl.when(r != NL - 1)
    def _():
        for m in range(3):
            base_copy(m).wait_send()
            for c in range(2):
                level_copy(m, c).wait_send()
        for s in range(QUAD):
            arr_copy(s).wait_send()
        for m in range(2):
            for c in range(QUAD):
                hop(m, c).wait_send()

    @pl.when(r < GROUP - 1)
    def _():
        for s in range(QUAD):
            far_copy(s).wait_send()

    @pl.when(first_half)
    def _():
        q_copy.wait_send()

    for s in range(QUAD):
        @pl.when(owner(s) != NL - 1)
        def _():
            first_copy(s, spot).wait_send()

    for tile in range(4):
        for layer in range(LD):
            out_copy(tile, layer).wait()


def per_device(weights, biases, guesses):
    f32, bf16 = jnp.float32, jnp.bfloat16
    dma = pltpu.SemaphoreType.DMA
    hbm = pl.BlockSpec(memory_space=pltpu.HBM)
    scratch = dict(
        wf=pltpu.VMEM((LD, D, D), bf16),
        bias=pltpu.VMEM((LD, D), f32),
        natural=pltpu.VMEM((D // LANES, ROWS, LANES), f32),
        guess=pltpu.VMEM((GROUP, PR, D), f32),
        base_in=pltpu.VMEM((3, PR, D), f32),
        tau=pltpu.VMEM((GROUP, PR, D), f32),
        inc_in=pltpu.VMEM((3, PR, D), bf16),
        inc_out=pltpu.VMEM((4, PR, D), bf16),
        heads=pltpu.VMEM((QUAD, D, D), bf16),
        hbias=pltpu.VMEM((QUAD, LD, D), f32),
        part=pltpu.VMEM((QUAD, QR, D), f32),
        part_act=pltpu.VMEM((QUAD, QR, D), f32),
        arr=pltpu.VMEM((QUAD, QR, D), bf16),
        base_far=pltpu.VMEM((QR, D), f32),
        coarse_in=pltpu.VMEM((QR, D), f32),
        coarse_out=pltpu.VMEM((QR, D), f32),
        coarse=pltpu.VMEM((QUAD, QR, D), f32),
        corr_in=pltpu.VMEM((PR, D), f32),
        first_out=pltpu.VMEM((QUAD, QR, D), f32),
        first_in=pltpu.VMEM((PR, D), f32),
        hop_in=pltpu.VMEM((2, PR, D), f32),
        hop_out=pltpu.VMEM((2, PR, D), f32),
        fin=pltpu.VMEM((LD, D // LANES, ROWS, LANES), f32),
        first_now=pltpu.VMEM((PR, D), f32),
        load_s=dma((LD + 1 + D // LANES,)),
        ring_s=dma((2, 8, LD)), ring_r=dma((2, 8, LD)),
        head_s=dma((QUAD, NZ)), head_r=dma((QUAD, NZ)),
        bias_s=dma((QUAD,)), bias_r=dma((QUAD,)),
        part_s=dma((QUAD,)), part_r=dma((QUAD,)),
        base_s=dma((3,)), base_r=dma((3,)),
        far_s=dma((QUAD,)), far_r=dma((1,)),
        level_s=dma((3, 2)), level_r=dma((3, 2)),
        arr_s=dma((QUAD,)), arr_r=dma((QUAD,)),
        q_s=dma((1,)), q_r=dma((1,)),
        corr_s=dma((QUAD,)), corr_r=dma((QUAD,)),
        first_s=dma((QUAD,)), first_r=dma((QUAD,)),
        hop_s=dma((2, QUAD)), hop_r=dma((2, QUAD)),
        own_s=dma((1,)),
        done=pltpu.VMEM((LD, ROWS, D), bf16),
        out_s=dma((4, LD)),
    )
    return pl.pallas_call(
        kernel,
        out_shape=jax.ShapeDtypeStruct((LD, ROWS, D), bf16),
        in_specs=[hbm, hbm, hbm],
        out_specs=hbm,
        scratch_shapes=scratch,
        compiler_params=pltpu.CompilerParams(
            collective_id=1, has_side_effects=True, vmem_limit_bytes=56 * 2**20),
        cost_estimate=pl.CostEstimate(flops=3 * 10**9, bytes_accessed=3 * 2**20, transcendentals=3 * 10**6),
    )(weights, biases, guesses)


def solution(mesh):
    in_specs = (P("layer", "dp", None), P("layer", None), P("layer", "dp", None))
    out_specs = P("layer", "dp", None)
    return jax.shard_map(
        per_device, mesh=mesh, in_specs=in_specs, out_specs=out_specs, check_vma=False
    )
```

```python
import jax
import jax.numpy as jnp
from jax import lax
from jax.experimental import pallas as pl
from jax.experimental.pallas import tpu as pltpu
from jax.sharding import PartitionSpec as P

MESH = pl.DeviceIdType.MESH
GROUP = 4
QUAD = 4
NL = 32
NZ = 16
D = 512
LANES = 128
ROWS = 512
PR = ROWS // GROUP
HR = PR // 2
QR = PR // QUAD
KR = D // NZ
LD = 4
FINE = 4.0 / 128
BLOCK = 4 * FINE
WIDE = 16 * FINE


def kernel(
    w_ref, b_ref, g_ref, o_ref,
    wf, bias, natural, guess, base_in, tau, inc_in, inc_out, heads, hbias, part, part_act, arr, base_far,
    coarse_in, coarse_out, coarse, corr_in, first_out, first_in, hop_in, hop_out, fin, first_now,
    load_s, ring_s, ring_r, head_s, head_r, bias_s, bias_r, part_s, part_r, base_s, base_r, far_s, far_r,
    level_s, level_r, arr_s, arr_r, q_s, q_r, corr_s, corr_r, first_s, first_r, hop_s, hop_r, own_s, done, out_s,
):
    r = lax.axis_index("layer")
    z = lax.axis_index("dp")
    nxt = lax.rem(r + 1, NL)
    prv = lax.rem(r + NL - 1, NL)
    spot = lax.rem(r // 4, QUAD)
    spot_next = lax.rem(nxt // 4, QUAD)
    first_half = r < 16
    turn = 2 * (r // 16)
    turn_next = 2 * (nxt // 16)
    outer = lax.rem(spot // 2 + r // 16, 2)
    far = lax.rem(r + 24 - 16 * outer + (r // 16) * (32 * outer - 16), NL)
    starts = jnp.logical_and(first_half, lax.rem(r, GROUP) == 0)
    starts_later = jnp.logical_and(first_half, lax.rem(r, GROUP) != 0)

    def phase(back):
        return lax.rem(r - back + 2 * GROUP, GROUP)

    def to(layer, src, dst, send, recv):
        return pltpu.make_async_remote_copy(
            src_ref=src, dst_ref=dst, send_sem=send, recv_sem=recv,
            device_id=(layer, z), device_id_type=MESH)

    loads = [
        pltpu.make_async_copy(
            w_ref.at[layer], wf.at[layer, pl.ds(pl.multiple_of(z * KR, KR), KR)], load_s.at[layer])
        for layer in range(LD)
    ]
    loads.append(pltpu.make_async_copy(b_ref, bias, load_s.at[LD]))
    guess_loads = [
        pltpu.make_async_copy(g_ref.at[0, :, pl.ds(c * LANES, LANES)], natural.at[c], load_s.at[LD + 1 + c])
        for c in range(D // LANES)
    ]
    for load in loads + guess_loads:
        load.start()

    def peer(d, i):
        j = lax.rem(d // 4, QUAD)
        other = j + 1 - 2 * lax.rem(j, 2) if i == 1 else lax.rem(j + 2, 4) if i == 2 else 3 - j
        return d + 4 * (other - j)

    barrier = pltpu.get_barrier_semaphore()
    greeted = [(r, lax.rem(z + d, NZ)) for d in (1, NZ - 1)]
    greeted += [(nxt, z), (prv, z), (far, z)]
    for i in range(1, QUAD):
        greeted += [
            (peer(r, i), z),
            (lax.rem(peer(r, i) + 1, NL), z), (peer(prv, i), z),
            (peer(nxt, i), z), (lax.rem(peer(r, i) + NL - 1, NL), z),
        ]
    for dev in greeted:
        pl.semaphore_signal(barrier, inc=1, device_id=dev, device_id_type=MESH)
    for load in loads:
        load.wait()
    pl.semaphore_wait(barrier, len(greeted))

    def shard(layer, origin):
        o = lax.rem(origin + 2 * NZ, NZ)
        return wf.at[layer, pl.ds(pl.multiple_of(o * KR, KR), KR)]

    def ring(way, step, layer, arrived=False):
        back = step if arrived else step - 1
        block = shard(layer, z - back if way == 0 else z + back)
        return pltpu.make_async_remote_copy(
            src_ref=block, dst_ref=block, send_sem=ring_s.at[way, step - 1, layer],
            recv_sem=ring_r.at[way, step - 1, layer],
            device_id=(r, lax.rem(z + (1 if way == 0 else NZ - 1), NZ)), device_id_type=MESH)

    def owner(s):
        return r + 4 * (s - spot)

    def each_peer(action):
        for s in range(QUAD):
            @pl.when(s != spot)
            def _():
                action(s)

    def head_copy(s, slot, origin):
        o = lax.rem(origin + 2 * NZ, NZ)
        rows = pl.ds(pl.multiple_of(o * KR, KR), KR)
        return to(owner(s), wf.at[0, rows], heads.at[slot, rows], head_s.at[s, o], head_r.at[slot, o])

    mate = spot + 1 - 2 * lax.rem(spot, 2)
    across = lax.rem(spot + 2, QUAD)
    diagonal = 3 - spot

    def send_head(origin):
        head_copy(mate, spot, origin).start()
        head_copy(across, spot, origin).start()

    def head_hand_on(origin):
        o = lax.rem(origin + 2 * NZ, NZ)
        rows = pl.ds(pl.multiple_of(o * KR, KR), KR)
        return to(
            owner(across), heads.at[mate, rows], heads.at[mate, rows], head_s.at[diagonal, o], head_r.at[mate, o])

    def hand_on(origin):
        head_copy(mate, mate, origin).wait_recv()
        head_hand_on(origin).start()

    def bias_copy(s, slot):
        return to(owner(s), bias, hbias.at[slot], bias_s.at[s], bias_r.at[slot])

    def quarter(j):
        if not isinstance(j, int):
            return pl.ds(pl.multiple_of(j * QR, QR), QR)
        return pl.ds(j * QR, QR)

    def part_copy(s, slot):
        return to(owner(s), guess.at[phase(0), quarter(lax.rem(s + turn, QUAD))], part.at[slot], part_s.at[s], part_r.at[slot])

    def base_copy(m):
        src = guess.at[phase(0)] if m == 0 else base_in.at[m - 1]
        return to(nxt, src, base_in.at[m], base_s.at[m], base_r.at[m])

    def last_step(way, layer):
        return (layer < 2) == (way == 0)

    for layer in range(LD):
        for way in range(2):
            ring(way, 1, layer).start()
    send_head(z)
    each_peer(lambda s: bias_copy(s, spot).start())
    for c in range(D // LANES):
        guess_loads[c].wait()
        for p in range(GROUP):
            guess[p, :, pl.ds(c * LANES, LANES)] = natural[c, pl.ds(p, PR, stride=GROUP), :]

    @pl.when(r != NL - 1)
    def _():
        base_copy(0).start()

    each_peer(lambda s: part_copy(s, spot).start())
    rows_here = lax.rem(spot + turn, QUAD)
    part[spot] = guess[phase(0), quarter(rows_here), :]
    hbias[spot] = bias[...]

    @pl.when(r == 0)
    def _():
        for m in range(1, 4):
            base_in[m - 1] = guess[phase(m)]
            inc_in[m - 1] = jnp.zeros((PR, D), jnp.bfloat16)
        first_in[...] = guess[phase(1)].astype(jnp.bfloat16)
        hop_in[0] = guess[phase(2)].astype(jnp.bfloat16)
        hop_in[1] = guess[phase(3)].astype(jnp.bfloat16)

    def ring_body(step, carry):
        for layer in range(LD):
            for way in range(2):
                ring(way, step, layer, True).wait_recv()
                ring(way, step + 1, layer).start()
                if layer == 0:
                    send_head(z - step if way == 0 else z + step)
        return carry

    def ring_and_hand_on(step, carry):
        ring_body(step, carry)
        hand_on(z - step + 3)

        @pl.when(step > 3)
        def _():
            hand_on(z + step - 3)

        return carry

    def far_copy(s):
        return to(nxt + 4 * s, base_in.at[2, quarter(s)], base_far, far_s.at[s], far_r.at[0])

    for m in range(3):
        lax.fori_loop(1 + 2 * m, 3 + 2 * m, ring_body if m == 0 else ring_and_hand_on, 0)

        @pl.when(r != 0)
        def _():
            base_copy(m).wait_recv()

        if m < 2:
            @pl.when(r != NL - 1)
            def _():
                base_copy(m + 1).start()
        else:
            @pl.when(r < GROUP - 1)
            def _():
                for s in range(QUAD):
                    far_copy(s).start()

    for layer in range(LD):
        for way in range(2):
            ring(way, 7, layer, True).wait_recv()
            if last_step(way, layer):
                ring(way, 8, layer).start()
            if layer == 0:
                send_head(z - 7 if way == 0 else z + 7)

    hand_on(z - 4)
    hand_on(z + 4)

    def finish(layer):
        way = 0 if layer < 2 else 1
        ring(way, 8, layer, True).wait_recv()

    def act(u, weight, row):
        return jnp.tanh(jnp.dot(u.astype(jnp.bfloat16), weight, preferred_element_type=jnp.float32) + row)

    def bias_row(layer):
        return bias[pl.ds(layer, 1), :]

    finish(0)
    send_head(z - 8)
    own_head = pltpu.make_async_copy(wf.at[0], heads.at[spot], own_s.at[0])
    own_head.start()

    def sweep(back, first_time=False):
        p = phase(back)
        start = guess[p]
        first = act(start, wf[0], bias_row(0))
        inc = FINE * first
        for layer in range(1, LD):
            if first_time:
                finish(layer)
            inc = inc + FINE * act(start + inc, wf[layer], bias_row(layer))
        tau[p] = inc - BLOCK * first
        return inc

    def chunk(c):
        return pl.ds(c * HR, HR)

    def level_copy(m, c):
        return to(nxt, inc_out.at[m, chunk(c)], inc_in.at[m, chunk(c)], level_s.at[m, c], level_r.at[m, c])

    inc_out[0] = sweep(0, True).astype(jnp.bfloat16)

    @pl.when(r != NL - 1)
    def _():
        for c in range(2):
            level_copy(0, c).start()


    def arr_copy(s):
        return to(
            nxt + 4 * (lax.rem(s + turn_next, QUAD) - spot_next), inc_out.at[3, quarter(s)], arr.at[spot_next], arr_s.at[s], arr_r.at[spot_next])

    for m in range(1, 4):
        sweep(m)
        p = phase(m)
        for c in range(2):
            @pl.when(r != 0)
            def _():
                level_copy(m - 1, c).wait_recv()

            before = inc_in[m - 1, chunk(c), :].astype(jnp.float32)
            u = base_in[m - 1, chunk(c), :] + before
            after = before + BLOCK * act(u, wf[0], bias_row(0)) + tau[p, chunk(c), :]
            inc_out[m, chunk(c), :] = after.astype(jnp.bfloat16)

            @pl.when(r != NL - 1)
            def _():
                if m < 3:
                    level_copy(m, c).start()
                else:
                    arr_copy(2 * c).start()
                    arr_copy(2 * c + 1).start()

        if m == 1:
            for back in (5, 6):
                hand_on(z - back)
                hand_on(z + back)
        elif m == 2:
            hand_on(z - 7)
            hand_on(z + 7)
            hand_on(z - 8)

    own_head.wait()

    def wait_from(s):
        def wait_head(o, carry):
            head_copy(s, s, o).wait_recv()
            return carry

        @pl.when(s != mate)
        def _():
            lax.fori_loop(0, NZ, wait_head, 0)

        bias_copy(s, s).wait_recv()
        part_copy(s, s).wait_recv()

    each_peer(wait_from)
    for s in range(QUAD):
        part_act[s] = act(part[s], heads[s], hbias[s, pl.ds(0, 1), :])

    def arrived(s):
        to(nxt, inc_out.at[3, quarter(s)], arr.at[s], arr_s.at[s], arr_r.at[s]).wait_recv()

    q_copy = to(far, coarse_out, coarse_in, q_s.at[0], q_r.at[0])

    @pl.when(starts)
    def _():
        coarse[0] = part[0]

    @pl.when(starts_later)
    def _():
        far_copy(0).wait_recv()
        arrived(0)
        coarse[0] = base_far[...] + arr[0].astype(jnp.float32)

    @pl.when(jnp.logical_not(first_half))
    def _():
        arrived(0)

    for s in range(1, QUAD):
        arrived(s)

    @pl.when(jnp.logical_not(first_half))
    def _():
        q_copy.wait_recv()
        coarse[0] = coarse_in[...] + arr[0].astype(jnp.float32)

    def first_copy(s, place):
        return to(
            lax.rem(owner(s) + 1, NL), first_out.at[s], first_in.at[quarter(place)], first_s.at[s], first_r.at[place])

    def corr_copy(s, place):
        return to(owner(s), coarse.at[s], corr_in.at[quarter(place)], corr_s.at[s], corr_r.at[place])

    u = coarse[0]
    for s in range(QUAD):
        change = act(u, heads[s], hbias[s, pl.ds(0, 1), :]) - part_act[s]
        following = u + WIDE * change
        if s == QUAD - 1:
            @pl.when(first_half)
            def _():
                coarse_out[...] = following
                q_copy.start()

        first_out[s] = (u + BLOCK * change).astype(jnp.bfloat16)

        @pl.when(jnp.logical_and(jnp.logical_not(first_half), owner(s) != NL - 1))
        def _():
            first_copy(s, rows_here).start()

        if s < QUAD - 1:
            u = following + arr[s + 1].astype(jnp.float32)
            coarse[s + 1] = u

    for s in range(QUAD):
        @pl.when(first_half)
        def _():
            first_copy(s, rows_here).start()

    each_peer(lambda s: corr_copy(s, rows_here).start())

    def put(layer, p, values):
        for c in range(D // LANES):
            fin[layer, c, pl.ds(p, PR, stride=GROUP), :] = values[:, c * LANES:(c + 1) * LANES]

    def settle(back, u):
        for layer in range(LD):
            u = u + FINE * act(u, wf[layer], bias_row(layer))
            put(layer, phase(back), u)

    corr_in[quarter(rows_here), :] = coarse[spot]

    def hop(m, c):
        return to(nxt, hop_out.at[m, quarter(c)], hop_in.at[m, quarter(c)], hop_s.at[m, c], hop_r.at[m, c])

    for m in range(1, 4):
        p = phase(m)
        for c in range(QUAD):
            @pl.when(r != 0)
            def _():
                if m == 1:
                    first_copy(0, c).wait_recv()
                else:
                    hop(m - 2, c).wait_recv()

            if m == 1:
                u = first_in[quarter(c), :].astype(jnp.float32) + inc_in[0, quarter(c), :].astype(jnp.float32)
                first_now[quarter(c), :] = u
            elif m == 2:
                u = hop_in[0, quarter(c), :].astype(jnp.float32)
            if m < 3:
                after = u + BLOCK * act(u, wf[0], bias_row(0)) + tau[p, quarter(c), :]
                hop_out[m - 1, quarter(c), :] = after.astype(jnp.bfloat16)

                @pl.when(r != NL - 1)
                def _():
                    hop(m - 1, c).start()

        if m == 1:
            settle(1, first_now[...])
        else:
            settle(m, hop_in[m - 2].astype(jnp.float32))
        if m == 2:
            each_peer(lambda s: corr_copy(s, lax.rem(s + turn, QUAD)).wait_recv())
            settle(0, corr_in[...])

    def out_copy(tile, layer):
        rows = pl.ds(tile * 128, 128)
        return pltpu.make_async_copy(done.at[layer, rows], o_ref.at[layer, rows], out_s.at[tile, layer])

    for layer in range(LD):
        for tile in range(4):
            rows = pl.ds(tile * 128, 128)
            for c in range(D // LANES):
                done[layer, rows, pl.ds(c * LANES, LANES)] = fin[layer, c, rows, :].astype(jnp.bfloat16)
            out_copy(tile, layer).start()

    def drain(step, carry):
        for layer in range(LD):
            for way in range(2):
                ring(way, step, layer).wait_send()
        return carry

    lax.fori_loop(1, 8, drain, 0)
    for layer in range(LD):
        for way in range(2):
            if last_step(way, layer):
                ring(way, 8, layer).wait_send()

    def drain_peer(s):
        def drain_head(o, carry):
            head_copy(s, spot, o).wait_send()
            return carry

        lax.fori_loop(0, NZ, drain_head, 0)
        bias_copy(s, spot).wait_send()
        part_copy(s, spot).wait_send()
        corr_copy(s, rows_here).wait_send()

    each_peer(drain_peer)

    @pl.when(r != NL - 1)
    def _():
        for m in range(3):
            base_copy(m).wait_send()
            for c in range(2):
                level_copy(m, c).wait_send()
        for s in range(QUAD):
            arr_copy(s).wait_send()
        for m in range(2):
            for c in range(QUAD):
                hop(m, c).wait_send()

    @pl.when(r < GROUP - 1)
    def _():
        for s in range(QUAD):
            far_copy(s).wait_send()

    @pl.when(first_half)
    def _():
        q_copy.wait_send()

    for s in range(QUAD):
        @pl.when(owner(s) != NL - 1)
        def _():
            first_copy(s, rows_here).wait_send()

    for tile in range(4):
        for layer in range(LD):
            out_copy(tile, layer).wait()


def per_device(weights, biases, guesses):
    f32, bf16 = jnp.float32, jnp.bfloat16
    dma = pltpu.SemaphoreType.DMA
    hbm = pl.BlockSpec(memory_space=pltpu.HBM)
    scratch = dict(
        wf=pltpu.VMEM((LD, D, D), bf16),
        bias=pltpu.VMEM((LD, D), f32),
        natural=pltpu.VMEM((D // LANES, ROWS, LANES), f32),
        guess=pltpu.VMEM((GROUP, PR, D), f32),
        base_in=pltpu.VMEM((3, PR, D), f32),
        tau=pltpu.VMEM((GROUP, PR, D), f32),
        inc_in=pltpu.VMEM((3, PR, D), bf16),
        inc_out=pltpu.VMEM((4, PR, D), bf16),
        heads=pltpu.VMEM((QUAD, D, D), bf16),
        hbias=pltpu.VMEM((QUAD, LD, D), f32),
        part=pltpu.VMEM((QUAD, QR, D), f32),
        part_act=pltpu.VMEM((QUAD, QR, D), f32),
        arr=pltpu.VMEM((QUAD, QR, D), bf16),
        base_far=pltpu.VMEM((QR, D), f32),
        coarse_in=pltpu.VMEM((QR, D), f32),
        coarse_out=pltpu.VMEM((QR, D), f32),
        coarse=pltpu.VMEM((QUAD, QR, D), f32),
        corr_in=pltpu.VMEM((PR, D), f32),
        first_out=pltpu.VMEM((QUAD, QR, D), bf16),
        first_in=pltpu.VMEM((PR, D), bf16),
        hop_in=pltpu.VMEM((2, PR, D), bf16),
        hop_out=pltpu.VMEM((2, PR, D), bf16),
        fin=pltpu.VMEM((LD, D // LANES, ROWS, LANES), f32),
        first_now=pltpu.VMEM((PR, D), f32),
        load_s=dma((LD + 1 + D // LANES,)),
        ring_s=dma((2, 8, LD)), ring_r=dma((2, 8, LD)),
        head_s=dma((QUAD, NZ)), head_r=dma((QUAD, NZ)),
        bias_s=dma((QUAD,)), bias_r=dma((QUAD,)),
        part_s=dma((QUAD,)), part_r=dma((QUAD,)),
        base_s=dma((3,)), base_r=dma((3,)),
        far_s=dma((QUAD,)), far_r=dma((1,)),
        level_s=dma((3, 2)), level_r=dma((3, 2)),
        arr_s=dma((QUAD,)), arr_r=dma((QUAD,)),
        q_s=dma((1,)), q_r=dma((1,)),
        corr_s=dma((QUAD,)), corr_r=dma((QUAD,)),
        first_s=dma((QUAD,)), first_r=dma((QUAD,)),
        hop_s=dma((2, QUAD)), hop_r=dma((2, QUAD)),
        own_s=dma((1,)),
        done=pltpu.VMEM((LD, ROWS, D), bf16),
        out_s=dma((4, LD)),
    )
    return pl.pallas_call(
        kernel,
        out_shape=jax.ShapeDtypeStruct((LD, ROWS, D), bf16),
        in_specs=[hbm, hbm, hbm],
        out_specs=hbm,
        scratch_shapes=scratch,
        compiler_params=pltpu.CompilerParams(
            collective_id=1, has_side_effects=True, vmem_limit_bytes=56 * 2**20),
        cost_estimate=pl.CostEstimate(flops=3 * 10**9, bytes_accessed=3 * 2**20, transcendentals=3 * 10**6),
    )(weights, biases, guesses)


def solution(mesh):
    in_specs = (P("layer", "dp", None), P("layer", None), P("layer", "dp", None))
    out_specs = P("layer", "dp", None)
    return jax.shard_map(
        per_device, mesh=mesh, in_specs=in_specs, out_specs=out_specs, check_vma=False
    )
```

```python
import jax
import jax.numpy as jnp
from jax import lax
from jax.experimental import pallas as pl
from jax.experimental.pallas import tpu as pltpu
from jax.sharding import PartitionSpec as P

MESH = pl.DeviceIdType.MESH
GROUP = 4
QUAD = 4
NL = 32
NZ = 16
D = 512
LANES = 128
ROWS = 512
PR = ROWS // GROUP
HR = PR // 2
QR = PR // QUAD
KR = D // NZ
LD = 4
FINE = 4.0 / 128
BLOCK = 4 * FINE
WIDE = 16 * FINE


def kernel(
    w_ref, b_ref, g_ref, o_ref,
    wf, bias, natural, guess, base_in, tau, inc_in, inc_out, heads, hbias, part, part_act, arr, base_far,
    coarse_in, coarse_out, coarse, corr_in, first_out, first_in, hop_in, hop_out, fin, first_now,
    load_s, ring_s, ring_r, head_s, head_r, bias_s, bias_r, part_s, part_r, base_s, base_r, far_s, far_r,
    level_s, level_r, arr_s, arr_r, q_s, q_r, corr_s, corr_r, first_s, first_r, hop_s, hop_r, own_s, done, out_s,
):
    r = lax.axis_index("layer")
    z = lax.axis_index("dp")
    nxt = lax.rem(r + 1, NL)
    prv = lax.rem(r + NL - 1, NL)
    spot = lax.rem(r // 4, QUAD)
    spot_next = lax.rem(nxt // 4, QUAD)
    first_half = r < 16
    turn = 2 * (r // 16)
    turn_next = 2 * (nxt // 16)
    outer = lax.rem(spot // 2 + r // 16, 2)
    far = lax.rem(r + 24 - 16 * outer + (r // 16) * (32 * outer - 16), NL)
    starts = jnp.logical_and(first_half, lax.rem(r, GROUP) == 0)
    starts_later = jnp.logical_and(first_half, lax.rem(r, GROUP) != 0)

    def phase(back):
        return lax.rem(r - back + 2 * GROUP, GROUP)

    def to(layer, src, dst, send, recv):
        return pltpu.make_async_remote_copy(
            src_ref=src, dst_ref=dst, send_sem=send, recv_sem=recv,
            device_id=(layer, z), device_id_type=MESH)

    loads = [
        pltpu.make_async_copy(
            w_ref.at[layer], wf.at[layer, pl.ds(pl.multiple_of(z * KR, KR), KR)], load_s.at[layer])
        for layer in range(LD)
    ]
    loads.append(pltpu.make_async_copy(b_ref, bias, load_s.at[LD]))
    guess_loads = [
        pltpu.make_async_copy(g_ref.at[0, :, pl.ds(c * LANES, LANES)], natural.at[c], load_s.at[LD + 1 + c])
        for c in range(D // LANES)
    ]
    for load in loads + guess_loads:
        load.start()

    def peer(d, i):
        j = lax.rem(d // 4, QUAD)
        other = j + 1 - 2 * lax.rem(j, 2) if i == 1 else lax.rem(j + 2, 4) if i == 2 else 3 - j
        return d + 4 * (other - j)

    barrier = pltpu.get_barrier_semaphore()
    greeted = [(r, lax.rem(z + d, NZ)) for d in (1, NZ - 1)]
    greeted += [(nxt, z), (prv, z), (far, z)]
    for i in range(1, QUAD):
        greeted += [
            (peer(r, i), z),
            (lax.rem(peer(r, i) + 1, NL), z), (peer(prv, i), z),
            (peer(nxt, i), z), (lax.rem(peer(r, i) + NL - 1, NL), z),
        ]
    for dev in greeted:
        pl.semaphore_signal(barrier, inc=1, device_id=dev, device_id_type=MESH)
    for load in loads:
        load.wait()
    pl.semaphore_wait(barrier, len(greeted))

    def shard(layer, origin):
        o = lax.rem(origin + 2 * NZ, NZ)
        return wf.at[layer, pl.ds(pl.multiple_of(o * KR, KR), KR)]

    def ring(way, step, layer, arrived=False):
        back = step if arrived else step - 1
        block = shard(layer, z - back if way == 0 else z + back)
        return pltpu.make_async_remote_copy(
            src_ref=block, dst_ref=block, send_sem=ring_s.at[way, step - 1, layer],
            recv_sem=ring_r.at[way, step - 1, layer],
            device_id=(r, lax.rem(z + (1 if way == 0 else NZ - 1), NZ)), device_id_type=MESH)

    def owner(s):
        return r + 4 * (s - spot)

    def each_peer(action):
        for s in range(QUAD):
            @pl.when(s != spot)
            def _():
                action(s)

    def head_copy(s, slot, origin):
        o = lax.rem(origin + 2 * NZ, NZ)
        rows = pl.ds(pl.multiple_of(o * KR, KR), KR)
        return to(owner(s), wf.at[0, rows], heads.at[slot, rows], head_s.at[s, o], head_r.at[slot, o])

    mate = spot + 1 - 2 * lax.rem(spot, 2)
    across = lax.rem(spot + 2, QUAD)
    diagonal = 3 - spot

    def send_head(origin):
        head_copy(mate, spot, origin).start()
        head_copy(across, spot, origin).start()

    def head_hand_on(origin):
        o = lax.rem(origin + 2 * NZ, NZ)
        rows = pl.ds(pl.multiple_of(o * KR, KR), KR)
        return to(
            owner(across), heads.at[mate, rows], heads.at[mate, rows], head_s.at[diagonal, o], head_r.at[mate, o])

    def hand_on(origin):
        head_copy(mate, mate, origin).wait_recv()
        head_hand_on(origin).start()

    def bias_copy(s, slot):
        return to(owner(s), bias, hbias.at[slot], bias_s.at[s], bias_r.at[slot])

    def quarter(j):
        if not isinstance(j, int):
            return pl.ds(pl.multiple_of(j * QR, QR), QR)
        return pl.ds(j * QR, QR)

    def part_copy(s, slot):
        return to(owner(s), guess.at[phase(0), quarter(lax.rem(s + turn, QUAD))], part.at[slot], part_s.at[s], part_r.at[slot])

    def base_copy(m):
        src = guess.at[phase(0)] if m == 0 else base_in.at[m - 1]
        return to(nxt, src, base_in.at[m], base_s.at[m], base_r.at[m])

    def last_step(way, layer):
        return (layer < 2) == (way == 0)

    for layer in range(LD):
        for way in range(2):
            ring(way, 1, layer).start()
    send_head(z)
    each_peer(lambda s: bias_copy(s, spot).start())
    for c in range(D // LANES):
        guess_loads[c].wait()
        for p in range(GROUP):
            guess[p, :, pl.ds(c * LANES, LANES)] = natural[c, pl.ds(p, PR, stride=GROUP), :]

    @pl.when(r != NL - 1)
    def _():
        base_copy(0).start()

    each_peer(lambda s: part_copy(s, spot).start())
    rows_here = lax.rem(spot + turn, QUAD)
    part[spot] = guess[phase(0), quarter(rows_here), :]
    hbias[spot] = bias[...]

    @pl.when(r == 0)
    def _():
        for m in range(1, 4):
            base_in[m - 1] = guess[phase(m)]
            inc_in[m - 1] = jnp.zeros((PR, D), jnp.bfloat16)
        first_in[...] = guess[phase(1)].astype(jnp.bfloat16)
        hop_in[0] = guess[phase(2)].astype(jnp.bfloat16)
        hop_in[1] = guess[phase(3)].astype(jnp.bfloat16)

    def ring_body(step, carry):
        for layer in range(LD):
            for way in range(2):
                ring(way, step, layer, True).wait_recv()
                ring(way, step + 1, layer).start()
                if layer == 0:
                    send_head(z - step if way == 0 else z + step)
        return carry

    def ring_and_hand_on(step, carry):
        ring_body(step, carry)
        hand_on(z - step + 3)

        @pl.when(step > 3)
        def _():
            hand_on(z + step - 3)

        return carry

    def far_copy(s):
        return to(nxt + 4 * s, base_in.at[2, quarter(s)], base_far, far_s.at[s], far_r.at[0])

    for m in range(3):
        lax.fori_loop(1 + 2 * m, 3 + 2 * m, ring_body if m == 0 else ring_and_hand_on, 0)

        @pl.when(r != 0)
        def _():
            base_copy(m).wait_recv()

        if m < 2:
            @pl.when(r != NL - 1)
            def _():
                base_copy(m + 1).start()
        else:
            @pl.when(r < GROUP - 1)
            def _():
                for s in range(QUAD):
                    far_copy(s).start()

    for layer in range(LD):
        for way in range(2):
            ring(way, 7, layer, True).wait_recv()
            if last_step(way, layer):
                ring(way, 8, layer).start()
            if layer == 0:
                send_head(z - 7 if way == 0 else z + 7)

    hand_on(z - 4)
    hand_on(z + 4)

    def finish(layer):
        way = 0 if layer < 2 else 1
        ring(way, 8, layer, True).wait_recv()

    def act(u, weight, row):
        return jnp.tanh(jnp.dot(u.astype(jnp.bfloat16), weight, preferred_element_type=jnp.float32) + row)

    def bias_row(layer):
        return bias[pl.ds(layer, 1), :]

    finish(0)
    send_head(z - 8)
    own_head = pltpu.make_async_copy(wf.at[0], heads.at[spot], own_s.at[0])
    own_head.start()

    def sweep(back, first_time=False):
        p = phase(back)
        start = guess[p]
        first = act(start, wf[0], bias_row(0))
        inc = FINE * first
        for layer in range(1, LD):
            if first_time:
                finish(layer)
            inc = inc + FINE * act(start + inc, wf[layer], bias_row(layer))
        tau[p] = inc - BLOCK * first
        return inc

    def chunk(c):
        return pl.ds(c * QR, QR)

    def level_copy(m, c):
        return to(nxt, inc_out.at[m, chunk(c)], inc_in.at[m, chunk(c)], level_s.at[m, c], level_r.at[m, c])

    inc_out[0] = sweep(0, True).astype(jnp.bfloat16)

    @pl.when(r != NL - 1)
    def _():
        for c in range(QUAD):
            level_copy(0, c).start()


    def arr_copy(s):
        return to(
            nxt + 4 * (lax.rem(s + turn_next, QUAD) - spot_next), inc_out.at[3, quarter(s)], arr.at[spot_next], arr_s.at[s], arr_r.at[spot_next])

    for m in range(1, 4):
        sweep(m)
        p = phase(m)
        for c in range(QUAD):
            @pl.when(r != 0)
            def _():
                level_copy(m - 1, c).wait_recv()

            before = inc_in[m - 1, chunk(c), :].astype(jnp.float32)
            u = base_in[m - 1, chunk(c), :] + before
            after = before + BLOCK * act(u, wf[0], bias_row(0)) + tau[p, chunk(c), :]
            inc_out[m, chunk(c), :] = after.astype(jnp.bfloat16)

            @pl.when(r != NL - 1)
            def _():
                if m < 3:
                    level_copy(m, c).start()
                else:
                    arr_copy(c).start()

        if m == 1:
            for back in (5, 6):
                hand_on(z - back)
                hand_on(z + back)
        elif m == 2:
            hand_on(z - 7)
            hand_on(z + 7)
            hand_on(z - 8)

    own_head.wait()

    def wait_from(s):
        def wait_head(o, carry):
            head_copy(s, s, o).wait_recv()
            return carry

        @pl.when(s != mate)
        def _():
            lax.fori_loop(0, NZ, wait_head, 0)

        bias_copy(s, s).wait_recv()
        part_copy(s, s).wait_recv()

    each_peer(wait_from)
    for s in range(QUAD):
        part_act[s] = act(part[s], heads[s], hbias[s, pl.ds(0, 1), :])

    def arrived(s):
        to(nxt, inc_out.at[3, quarter(s)], arr.at[s], arr_s.at[s], arr_r.at[s]).wait_recv()

    q_copy = to(far, coarse_out, coarse_in, q_s.at[0], q_r.at[0])

    @pl.when(starts)
    def _():
        coarse[0] = part[0]

    @pl.when(starts_later)
    def _():
        far_copy(0).wait_recv()
        arrived(0)
        coarse[0] = base_far[...] + arr[0].astype(jnp.float32)

    @pl.when(jnp.logical_not(first_half))
    def _():
        arrived(0)

    for s in range(1, QUAD):
        arrived(s)

    @pl.when(jnp.logical_not(first_half))
    def _():
        q_copy.wait_recv()
        coarse[0] = coarse_in[...] + arr[0].astype(jnp.float32)

    def first_copy(s, place):
        return to(
            lax.rem(owner(s) + 1, NL), first_out.at[s], first_in.at[quarter(place)], first_s.at[s], first_r.at[place])

    def corr_copy(s, place):
        return to(owner(s), coarse.at[s], corr_in.at[quarter(place)], corr_s.at[s], corr_r.at[place])

    u = coarse[0]
    for s in range(QUAD):
        change = act(u, heads[s], hbias[s, pl.ds(0, 1), :]) - part_act[s]
        following = u + WIDE * change
        if s == QUAD - 1:
            @pl.when(first_half)
            def _():
                coarse_out[...] = following
                q_copy.start()

        first_out[s] = (u + BLOCK * change).astype(jnp.bfloat16)

        @pl.when(jnp.logical_and(jnp.logical_not(first_half), owner(s) != NL - 1))
        def _():
            first_copy(s, rows_here).start()

        if s < QUAD - 1:
            u = following + arr[s + 1].astype(jnp.float32)
            coarse[s + 1] = u

    for s in range(QUAD):
        @pl.when(first_half)
        def _():
            first_copy(s, rows_here).start()

    each_peer(lambda s: corr_copy(s, rows_here).start())

    def put(layer, p, values):
        for c in range(D // LANES):
            fin[layer, c, pl.ds(p, PR, stride=GROUP), :] = values[:, c * LANES:(c + 1) * LANES]

    def settle(back, u):
        for layer in range(LD):
            u = u + FINE * act(u, wf[layer], bias_row(layer))
            put(layer, phase(back), u)

    corr_in[quarter(rows_here), :] = coarse[spot]

    def hop(m, c):
        return to(nxt, hop_out.at[m, quarter(c)], hop_in.at[m, quarter(c)], hop_s.at[m, c], hop_r.at[m, c])

    for m in range(1, 4):
        p = phase(m)
        for c in range(QUAD):
            @pl.when(r != 0)
            def _():
                if m == 1:
                    first_copy(0, c).wait_recv()
                else:
                    hop(m - 2, c).wait_recv()

            if m == 1:
                u = first_in[quarter(c), :].astype(jnp.float32) + inc_in[0, quarter(c), :].astype(jnp.float32)
                first_now[quarter(c), :] = u
            elif m == 2:
                u = hop_in[0, quarter(c), :].astype(jnp.float32)
            if m < 3:
                after = u + BLOCK * act(u, wf[0], bias_row(0)) + tau[p, quarter(c), :]
                hop_out[m - 1, quarter(c), :] = after.astype(jnp.bfloat16)

                @pl.when(r != NL - 1)
                def _():
                    hop(m - 1, c).start()

        if m == 1:
            settle(1, first_now[...])
        else:
            settle(m, hop_in[m - 2].astype(jnp.float32))
        if m == 2:
            each_peer(lambda s: corr_copy(s, lax.rem(s + turn, QUAD)).wait_recv())
            settle(0, corr_in[...])

    def out_copy(tile, layer):
        rows = pl.ds(tile * 128, 128)
        return pltpu.make_async_copy(done.at[layer, rows], o_ref.at[layer, rows], out_s.at[tile, layer])

    for layer in range(LD):
        for tile in range(4):
            rows = pl.ds(tile * 128, 128)
            for c in range(D // LANES):
                done[layer, rows, pl.ds(c * LANES, LANES)] = fin[layer, c, rows, :].astype(jnp.bfloat16)
            out_copy(tile, layer).start()

    def drain(step, carry):
        for layer in range(LD):
            for way in range(2):
                ring(way, step, layer).wait_send()
        return carry

    lax.fori_loop(1, 8, drain, 0)
    for layer in range(LD):
        for way in range(2):
            if last_step(way, layer):
                ring(way, 8, layer).wait_send()

    def drain_peer(s):
        def drain_head(o, carry):
            head_copy(s, spot, o).wait_send()
            return carry

        lax.fori_loop(0, NZ, drain_head, 0)
        bias_copy(s, spot).wait_send()
        part_copy(s, spot).wait_send()
        corr_copy(s, rows_here).wait_send()

    each_peer(drain_peer)

    @pl.when(r != NL - 1)
    def _():
        for m in range(3):
            base_copy(m).wait_send()
            for c in range(QUAD):
                level_copy(m, c).wait_send()
        for s in range(QUAD):
            arr_copy(s).wait_send()
        for m in range(2):
            for c in range(QUAD):
                hop(m, c).wait_send()

    @pl.when(r < GROUP - 1)
    def _():
        for s in range(QUAD):
            far_copy(s).wait_send()

    @pl.when(first_half)
    def _():
        q_copy.wait_send()

    for s in range(QUAD):
        @pl.when(owner(s) != NL - 1)
        def _():
            first_copy(s, rows_here).wait_send()

    for tile in range(4):
        for layer in range(LD):
            out_copy(tile, layer).wait()


def per_device(weights, biases, guesses):
    f32, bf16 = jnp.float32, jnp.bfloat16
    dma = pltpu.SemaphoreType.DMA
    hbm = pl.BlockSpec(memory_space=pltpu.HBM)
    scratch = dict(
        wf=pltpu.VMEM((LD, D, D), bf16),
        bias=pltpu.VMEM((LD, D), f32),
        natural=pltpu.VMEM((D // LANES, ROWS, LANES), f32),
        guess=pltpu.VMEM((GROUP, PR, D), f32),
        base_in=pltpu.VMEM((3, PR, D), f32),
        tau=pltpu.VMEM((GROUP, PR, D), f32),
        inc_in=pltpu.VMEM((3, PR, D), bf16),
        inc_out=pltpu.VMEM((4, PR, D), bf16),
        heads=pltpu.VMEM((QUAD, D, D), bf16),
        hbias=pltpu.VMEM((QUAD, LD, D), f32),
        part=pltpu.VMEM((QUAD, QR, D), f32),
        part_act=pltpu.VMEM((QUAD, QR, D), f32),
        arr=pltpu.VMEM((QUAD, QR, D), bf16),
        base_far=pltpu.VMEM((QR, D), f32),
        coarse_in=pltpu.VMEM((QR, D), f32),
        coarse_out=pltpu.VMEM((QR, D), f32),
        coarse=pltpu.VMEM((QUAD, QR, D), f32),
        corr_in=pltpu.VMEM((PR, D), f32),
        first_out=pltpu.VMEM((QUAD, QR, D), bf16),
        first_in=pltpu.VMEM((PR, D), bf16),
        hop_in=pltpu.VMEM((2, PR, D), bf16),
        hop_out=pltpu.VMEM((2, PR, D), bf16),
        fin=pltpu.VMEM((LD, D // LANES, ROWS, LANES), f32),
        first_now=pltpu.VMEM((PR, D), f32),
        load_s=dma((LD + 1 + D // LANES,)),
        ring_s=dma((2, 8, LD)), ring_r=dma((2, 8, LD)),
        head_s=dma((QUAD, NZ)), head_r=dma((QUAD, NZ)),
        bias_s=dma((QUAD,)), bias_r=dma((QUAD,)),
        part_s=dma((QUAD,)), part_r=dma((QUAD,)),
        base_s=dma((3,)), base_r=dma((3,)),
        far_s=dma((QUAD,)), far_r=dma((1,)),
        level_s=dma((3, QUAD)), level_r=dma((3, QUAD)),
        arr_s=dma((QUAD,)), arr_r=dma((QUAD,)),
        q_s=dma((1,)), q_r=dma((1,)),
        corr_s=dma((QUAD,)), corr_r=dma((QUAD,)),
        first_s=dma((QUAD,)), first_r=dma((QUAD,)),
        hop_s=dma((2, QUAD)), hop_r=dma((2, QUAD)),
        own_s=dma((1,)),
        done=pltpu.VMEM((LD, ROWS, D), bf16),
        out_s=dma((4, LD)),
    )
    return pl.pallas_call(
        kernel,
        out_shape=jax.ShapeDtypeStruct((LD, ROWS, D), bf16),
        in_specs=[hbm, hbm, hbm],
        out_specs=hbm,
        scratch_shapes=scratch,
        compiler_params=pltpu.CompilerParams(
            collective_id=1, has_side_effects=True, vmem_limit_bytes=56 * 2**20),
        cost_estimate=pl.CostEstimate(flops=3 * 10**9, bytes_accessed=3 * 2**20, transcendentals=3 * 10**6),
    )(weights, biases, guesses)


def solution(mesh):
    in_specs = (P("layer", "dp", None), P("layer", None), P("layer", "dp", None))
    out_specs = P("layer", "dp", None)
    return jax.shard_map(
        per_device, mesh=mesh, in_specs=in_specs, out_specs=out_specs, check_vma=False
    )
```
